512 devices in a mesh: tok: 16 (over y, core), exp: 8 (over z), tp: 4 (over x).
Axes of the slice: x: 4, y: 8, z: 8, core: 2. Of those that a mesh axis runs over, the one named last changes fastest.
Arguments:
- tokens: bfloat16 [2048, 4096], P('tok'), may hold values from -6 to 6
- router_weight: bfloat16 [4096, 8], replicated, may hold values from -4 to 4
- gate_weight: bfloat16 [8, 4096, 8192], P('exp', None, ('tok', 'tp')), may hold values from -0.09375 to 0.09375
- up_weight: bfloat16 [8, 4096, 8192], P('exp', None, ('tok', 'tp')), may hold values from -0.09375 to 0.09375
- down_weight: bfloat16 [8, 8192, 4096], P('exp', 'tok', 'tp'), may hold values from -0.0625 to 0.0625
- assignments: int32 [2048, 2], P('tok'), may hold values from 0 to 7, all different within a row; in each aligned block of 128 rows (0 to 127, 128 to 255, ...) at most 48 rows name the same one
- limits: int32 [16, 8], P('tok'), may hold values from 24 to 48
Outputs:
- mixed_out: bfloat16 [2048, 4096], P(('tok', 'exp'), 'tp')
The draws below stay inside these ranges and needn't reach their ends.
Inputs may be any that keep to these rules, and one draw needn't show every extreme that they name: `assignments`: each row names 2 different experts; in each aligned block of 128 rows no expert is named by more than 48 rows.
All inputs are finite; a program needn't handle non-finite values.
Results may differ from the reference program's by a relative error of at most 0.024.
Values may be sent and summed in bfloat16 or wider, within the bound.
No kernel may reach another device: no remote copies, remote signals or barrier semaphores. Data moves between devices by JAX's collectives and lax.ppermute only.
A program may use at most 128 MiB of HBM per device.

```python
import math
import jax
import jax.numpy as jnp
import numpy as np
from jax import lax

D = 4096
FF = 8192
TOP = 2
ITERS = 4
TOK_DEV = 128
EXPERTS = 8
CAP = 48
TOKENS = 2048
N_TOK = 16


def draw_router_weight(key, part):
    key = jax.random.fold_in(key, 7)
    jitter_key = jax.random.fold_in(key, 0)
    jitter = jax.random.normal(jitter_key, (D, EXPERTS), jnp.float32) / math.sqrt(D)
    values = jitter
    return jnp.clip(values, -4.0, 4.0).astype(jnp.bfloat16)


def draw_limits(key, part):
    key = jax.random.fold_in(key, 11)
    first_key, second_key, third_key, fourth_key = jax.random.split(key, 4)
    base_values = jax.random.randint(first_key, (N_TOK, EXPERTS), CAP // 2, CAP + 1)
    full_flags = jax.random.randint(fourth_key, (N_TOK, EXPERTS), 0, 2)
    full_column = jax.random.randint(second_key, (N_TOK, 1), 0, EXPERTS)
    low_column = (full_column + jax.random.randint(third_key, (N_TOK, 1), 1, EXPERTS)) % EXPERTS
    columns = jnp.arange(EXPERTS, dtype=jnp.int32)[None, :]
    values = jnp.where(full_flags == 1, CAP, base_values)
    values = jnp.where(columns == low_column, CAP // 2, values)
    values = jnp.where(columns == full_column, CAP, values)
    return values.astype(jnp.int32)


def steps_of(stream_key, dims, cuts, smallest, top_value):
    def one(dim, parts):
        steps = jax.random.uniform(jax.random.fold_in(jax.random.fold_in(stream_key, 6), dim), (parts,), jnp.float32, smallest / len(cuts), top_value / len(cuts))
        return jnp.repeat(jnp.exp(steps), dims[dim] // parts).reshape((-1,) + (1,) * (len(dims) - dim - 1))

    factor_of = one(*cuts[0])
    for cut in cuts[1:]:
        factor_of = factor_of * one(*cut)
    return factor_of


def deal_out(stream_key, own, number, rows, amount, top, most, slope):
    order = jax.random.permutation(stream_key, amount)
    crowded, usual = shares(amount, rows * top, most, slope, True), shares(amount, rows * top, most, slope, False)
    places = jnp.arange(amount)

    def named(lengths, rotation):
        used = int((lengths > 0).sum())
        fixed = max(1, used // 4)
        moved = fixed + (places - fixed + rotation * (used - fixed)) % max(1, amount - fixed)
        return jnp.zeros((amount,), jnp.int32).at[order[jnp.where(places < fixed, places, moved)]].set(jnp.asarray(lengths, jnp.int32))

    lengths = jnp.where(number % 4 == 0, named(crowded, number // 4), named(usual, number - number // 4 - 1))
    mixed = jax.random.permutation(jax.random.fold_in(own, 3), amount)
    giver, taker = mixed[0:amount // 2 * 2:2], mixed[1:amount // 2 * 2:2]
    slack = jnp.minimum(lengths[giver] - 1, most - lengths[taker]) // 2
    slack = jnp.where((giver == order[0]) | (taker == order[0]) | (lengths[taker] == 0), 0, jnp.maximum(slack, 0))
    moved = jax.random.randint(jax.random.fold_in(own, 4), (amount // 2,), 0, 1 << 20) % (slack + 1)
    lengths = lengths.at[giver].add(-moved).at[taker].add(moved)
    items = jnp.searchsorted(jnp.cumsum(lengths), jnp.arange(rows * top), side="right").astype(jnp.int32)
    table = items.reshape(top, rows).T
    table = table[jax.random.permutation(jax.random.fold_in(own, 1), rows)]
    rotation = jax.random.randint(jax.random.fold_in(own, 2), (rows, 1), 0, top)
    return jnp.take_along_axis(table, (jnp.arange(top)[None, :] + rotation) % top, axis=1)


def shares(number_of, total, most, lean, full):
    weights = [(1 << 20) // math.isqrt(grade ** lean) + 1 for grade in range(1, number_of + 1)]
    largest = most if full else min(most, max(-(-total // number_of), total * weights[0] // sum(weights)))
    least = 1 if total - largest >= number_of - 1 else 0
    holding, surplus = [largest] + [least] * (number_of - 1), total - largest - least * (number_of - 1)
    while surplus > 0:
        movable = [i for i in range(1, number_of) if holding[i] < largest] or [i for i in range(1, number_of) if holding[i] < most]
        mass, budget = sum([weights[i] for i in movable]), surplus
        for i in movable:
            extra = min(most - holding[i], max(1, budget * weights[i] // mass), surplus)
            holding[i] = holding[i] + extra
            surplus = surplus - extra
    return np.array(holding)


def bell_draw(own_key, dims, scale, limit, cuts=(), held_as=jnp.bfloat16):
    level = steps_of(own_key, dims, cuts, -0.22, 0.18) if cuts else 1.0
    values = jax.random.normal(own_key, dims, jnp.float32) * scale * level
    return jnp.minimum(jnp.maximum(values, -limit), limit).astype(held_as)


def setup_inputs(seed: int = 0) -> dict:
    splits = jax.random.split(jax.random.key(seed), 8)
    tokens = bell_draw(splits[0], (TOKENS, D), 1.0, 6.0, ((0, 16),))
    router_weight = draw_router_weight(jax.random.fold_in(splits[7], 71), 0)
    gate_weight = bell_draw(splits[2], (EXPERTS, D, FF), D ** -0.5, 0.09375, ((0, 8), (2, 64)))
    up_weight = bell_draw(splits[3], (EXPERTS, D, FF), D ** -0.5, 0.09375, ((0, 8), (2, 64)))
    down_weight = bell_draw(splits[4], (EXPERTS, FF, D), FF ** -0.5, 0.0625, ((0, 8), (1, 16), (2, 4)))
    assignments_keys = jax.random.split(jax.random.fold_in(splits[5], 1), TOKENS // TOK_DEV)
    assignments_turns = jax.random.permutation(jax.random.fold_in(splits[5], 3), TOKENS // TOK_DEV)
    assignments = jax.vmap(lambda own, number: deal_out(jax.random.fold_in(splits[5], 2), own, number, TOK_DEV, EXPERTS, TOP, CAP, 2))(assignments_keys, assignments_turns).reshape((TOKENS, TOP))
    limits = draw_limits(jax.random.fold_in(splits[7], 71), 0)
    return {"tokens": tokens, "router_weight": router_weight, "gate_weight": gate_weight, "up_weight": up_weight, "down_weight": down_weight, "assignments": assignments, "limits": limits}


SOFT_CAP = 8.0


def row_balance(balanced):
    return balanced - jnp.log(jnp.sum(jnp.exp(balanced), axis=1, keepdims=True)) + math.log(TOP)


def reference(tokens, router_weight, gate_weight, up_weight, down_weight, assignments, limits):
    logits = jnp.dot(tokens, router_weight, preferred_element_type=jnp.float32)
    balanced = row_balance(SOFT_CAP * jnp.tanh(logits / SOFT_CAP))
    target_log = math.log(TOKENS * TOP / EXPERTS)
    for repeat in range(ITERS):
        column = jnp.sum(jnp.exp(balanced), axis=0, keepdims=True)
        balanced = row_balance(balanced - jnp.log(column) + target_log)
    shards = TOKENS // TOK_DEV
    expert_ids = jnp.arange(EXPERTS, dtype=jnp.int32)
    picked = (assignments[:, :, None] == expert_ids).astype(jnp.int32)
    per_row = jnp.sum(picked, axis=1, dtype=jnp.int32).reshape(shards, TOK_DEV, EXPERTS)
    before = (jnp.cumsum(per_row, axis=1, dtype=jnp.int32) - per_row).reshape(TOKENS, EXPERTS)
    slot_index = jnp.sum(picked * before[:, None, :], axis=2, dtype=jnp.int32).astype(jnp.int32)
    shard_ids = (jnp.arange(TOKENS, dtype=jnp.int32) // TOK_DEV)[:, None]
    retained = slot_index < limits[shard_ids, assignments]
    gate_values = jnp.where(retained, jnp.exp(jnp.take_along_axis(balanced, assignments, axis=1)), 0.0)
    positions = (shard_ids * CAP + slot_index).astype(jnp.int32)
    row_total = shards * CAP
    block_units = FF // N_TOK

    def expert_block(inputs):
        expert, w_gate, w_up, w_down = inputs
        routed = (assignments == expert) & retained
        placed = jnp.sum(jnp.where(routed, positions, 0), axis=1, dtype=jnp.int32).astype(jnp.int32)
        target = jnp.where(jnp.any(routed, axis=1), placed, row_total).astype(jnp.int32)
        routed_rows = jnp.zeros((row_total, D), jnp.bfloat16).at[target].set(tokens, mode="drop")
        gate_sum = jnp.dot(routed_rows, w_gate, preferred_element_type=jnp.float32)
        up_sum = jnp.dot(routed_rows, w_up, preferred_element_type=jnp.float32)
        hidden = (jax.nn.silu(gate_sum) * up_sum).astype(jnp.bfloat16)
        total = jnp.zeros((row_total, D), jnp.float32)
        for block in range(N_TOK):
            lo = block * block_units
            partial_sum = jnp.dot(hidden[:, lo:lo + block_units], w_down[lo:lo + block_units], preferred_element_type=jnp.float32).astype(jnp.bfloat16)
            total = total + lax.optimization_barrier(partial_sum).astype(jnp.float32)
        return total.astype(jnp.bfloat16)

    outputs = lax.map(expert_block, (expert_ids, gate_weight, up_weight, down_weight))
    values = outputs[assignments, jnp.minimum(positions, row_total - 1)].astype(jnp.float32)
    mixed_out = jnp.sum(gate_values[:, :, None] * values, axis=1)
    return mixed_out.astype(jnp.bfloat16)
```

```python
import functools
import math

import jax
import jax.numpy as jnp
from jax import lax
from jax.experimental import pallas as pl
from jax.experimental.pallas import tpu as pltpu
from jax.sharding import Mesh, PartitionSpec as P

TOP = 2
ITERS = 4
SOFT_CAP = 8.0
CORES = 2


def swap_cores(value):
    return lax.ppermute(value, "core", [(0, 1), (1, 0)])


def ffn_kernel(rows_ref, gate_ref, up_ref, gate2_ref, up2_ref, out_ref, acc_ref, acc2_ref):
    step = pl.program_id(0)
    rows = rows_ref[...]
    own = jnp.dot(
        rows,
        jnp.concatenate([gate_ref[...], up_ref[...]], axis=1),
        preferred_element_type=jnp.float32,
    )
    peer = jnp.dot(
        rows,
        jnp.concatenate([gate2_ref[...], up2_ref[...]], axis=1),
        preferred_element_type=jnp.float32,
    )

    @pl.when(step == 0)
    def _():
        acc_ref[...] = own
        acc2_ref[...] = peer

    @pl.when(step > 0)
    def _():
        acc_ref[...] += own
        acc2_ref[...] += peer

    @pl.when(step == pl.num_programs(0) - 1)
    def _():
        units = gate_ref.shape[1]
        for index, ref in enumerate((acc_ref, acc2_ref)):
            gate = ref[:, :units]
            hidden = gate / (1.0 + jnp.exp(-gate)) * ref[:, units:]
            out_ref[:, index * units : (index + 1) * units] = hidden.astype(out_ref.dtype)


def ffn(rows, gate, up, gate2, up2, chunk=1024):
    count, width = rows.shape
    units = gate.shape[1]
    weight = pl.BlockSpec((chunk, units), lambda k: (k, 0))
    return pl.pallas_call(
        ffn_kernel,
        grid=(width // chunk,),
        in_specs=[pl.BlockSpec((count, chunk), lambda k: (0, k))] + [weight] * 4,
        out_specs=pl.BlockSpec((count, 2 * units), lambda k: (0, 0)),
        out_shape=jax.ShapeDtypeStruct((count, 2 * units), jnp.bfloat16),
        scratch_shapes=[pltpu.VMEM((count, 2 * units), jnp.float32)] * 2,
        compiler_params=pltpu.CompilerParams(vmem_limit_bytes=24 << 20),
        cost_estimate=pl.CostEstimate(
            flops=8 * count * width * units,
            bytes_accessed=2 * count * width + 8 * width * units,
            transcendentals=2 * count * units,
        ),
        name="ffn",
    )(rows, gate, up, gate2, up2)


def down_kernel(hidden_ref, down_ref, down2_ref, out_ref, acc_ref):
    step = pl.program_id(0)
    part = jnp.dot(
        hidden_ref[0],
        jnp.concatenate([down_ref[...], down2_ref[...]], axis=0),
        preferred_element_type=jnp.float32,
    )

    @pl.when(step == 0)
    def _():
        acc_ref[...] = part

    @pl.when(step > 0)
    def _():
        acc_ref[...] += part

    @pl.when(step == pl.num_programs(0) - 1)
    def _():
        out_ref[...] = acc_ref[...].astype(out_ref.dtype)


def down(hidden, weight, weight2):
    parts, count, units = hidden.shape
    columns = weight.shape[1]
    block = pl.BlockSpec((units // 2, columns), lambda k: (k, 0))
    return pl.pallas_call(
        down_kernel,
        grid=(parts,),
        in_specs=[pl.BlockSpec((1, count, units), lambda k: (k, 0, 0)), block, block],
        out_specs=pl.BlockSpec((count, columns), lambda k: (0, 0)),
        out_shape=jax.ShapeDtypeStruct((count, columns), jnp.bfloat16),
        scratch_shapes=[pltpu.VMEM((count, columns), jnp.float32)],
        compiler_params=pltpu.CompilerParams(vmem_limit_bytes=24 << 20),
        cost_estimate=pl.CostEstimate(
            flops=2 * parts * count * units * columns,
            bytes_accessed=2 * parts * units * (count + columns) + 2 * count * columns,
            transcendentals=0,
        ),
        name="down",
    )(hidden, weight, weight2)


def weigh_kernel(parts_ref, pick_ref, gate_ref, out_ref):
    total = jnp.sum(parts_ref[...].astype(jnp.float32), axis=0).astype(jnp.bfloat16)
    chosen = jnp.dot(pick_ref[...], total, preferred_element_type=jnp.float32)
    out_ref[...] = (chosen * gate_ref[...]).astype(out_ref.dtype)


def weigh(parts, pick, gate):
    count = pick.shape[0]
    columns = parts.shape[2]
    return pl.pallas_call(
        weigh_kernel,
        out_shape=jax.ShapeDtypeStruct((count, columns), jnp.bfloat16),
        compiler_params=pltpu.CompilerParams(vmem_limit_bytes=24 << 20),
        cost_estimate=pl.CostEstimate(
            flops=2 * count * pick.shape[1] * columns,
            bytes_accessed=2 * parts.size + 2 * count * columns,
            transcendentals=0,
        ),
        name="weigh",
    )(parts, pick, gate)


def local(tokens, router_weight, gate_weight, up_weight, down_weight, assignments, limits):
    local_rows = tokens.shape[0]
    experts = router_weight.shape[1]
    rings = lax.axis_size("y")
    shards = rings * CORES
    owners = lax.axis_size("exp")
    capacity = min(local_rows, max(2, 3 * local_rows * TOP // (2 * experts)))
    out_rows = local_rows // owners
    target = local_rows * shards * TOP / experts
    owner = lax.axis_index("exp")

    hit = jnp.any(assignments == owner, axis=1)
    row_ids = jnp.arange(local_rows, dtype=jnp.int32)
    earlier = (row_ids[None, :] < row_ids[:, None]) & hit[None, :]
    slot = jnp.sum(earlier.astype(jnp.int32), axis=1)
    kept = hit & (slot < lax.dynamic_index_in_dim(limits[0], owner, keepdims=False))
    slot_ids = jnp.arange(capacity, dtype=jnp.int32)
    select = ((slot_ids[:, None] == slot[None, :]) & kept[None, :]).astype(jnp.bfloat16)
    expert_rows = jnp.dot(select, tokens, preferred_element_type=jnp.float32).astype(jnp.bfloat16)
    rows = lax.all_gather(expert_rows, "y", axis=0, tiled=True)

    w_gate, w_up, w_down, tokens2, expert_rows2 = lax.optimization_barrier(
        (gate_weight[0], up_weight[0], down_weight[0], tokens, expert_rows)
    )
    gate2, up2, down2 = swap_cores(w_gate), swap_cores(w_up), swap_cores(w_down)

    logits = lax.dot_general(
        router_weight, tokens2, (((0,), (1,)), ((), ())), preferred_element_type=jnp.float32
    )
    capped = SOFT_CAP * jnp.tanh(logits / SOFT_CAP)
    scores = lax.all_gather(capped, ("y", "core"), axis=0)
    weights = jnp.exp(scores)
    weights = weights * (TOP / jnp.sum(weights, axis=1, keepdims=True))
    for repeat in range(ITERS):
        weights = weights * (target / jnp.sum(weights, axis=(0, 2), keepdims=True))
        weights = weights * (TOP / jnp.sum(weights, axis=1, keepdims=True))
    shard = lax.axis_index("y") * CORES + lax.axis_index("core")
    own = lax.dynamic_slice(weights, (shard, owner, 0), (1, 1, local_rows)).reshape(local_rows)
    gate_value = jnp.where(kept, own, 0.0)[:, None]
    pick = ((slot_ids[None, :] == slot[:, None]) & kept[:, None]).astype(jnp.bfloat16)

    hidden = ffn(rows, w_gate, w_up, gate2, up2)
    full_hidden = lax.all_gather(hidden, "tp", axis=0)
    partial = down(full_hidden, w_down, down2)
    parts = lax.all_to_all(partial.reshape(rings, capacity, partial.shape[1]), "y", 0, 0)
    shares = weigh(parts, pick, gate_value)
    shares = lax.all_to_all(shares.reshape(owners, out_rows, shares.shape[1]), "exp", 0, 0)
    return jnp.sum(shares.astype(jnp.float32), axis=0).astype(jnp.bfloat16)


def solution(mesh):
    shape = mesh.devices.shape
    fine = Mesh(
        mesh.devices.reshape((shape[0] // CORES, CORES) + shape[1:]), ("y", "core", "exp", "tp")
    )
    tok = ("y", "core")
    placed = (
        P(tok, None),
        P(),
        P("exp", None, tok + ("tp",)),
        P("exp", None, tok + ("tp",)),
        P("exp", tok, "tp"),
        P(tok, None),
        P(tok, None),
    )
    return jax.shard_map(
        local, mesh=fine, in_specs=placed, out_specs=P(tok + ("exp",), "tp"), check_vma=False
    )
```

```python
import jax
import jax.numpy as jnp
from jax import lax
from jax.experimental import pallas as pl
from jax.experimental.pallas import tpu as pltpu
from jax.sharding import Mesh, PartitionSpec as P

TOP = 2
ITERS = 4
SOFT_CAP = 8.0
CORES = 2


def swap_cores(value):
    return lax.ppermute(value, "core", [(0, 1), (1, 0)])


def route_kernel(owner_ref, limits_ref, assign_ref, tokens_ref, select_ref, rows_ref):
    owner = owner_ref[0]
    count = assign_ref.shape[1]
    capacity = select_ref.shape[0]
    hit = jnp.sum(jnp.where(assign_ref[...] == owner, 1.0, 0.0), axis=0, keepdims=True)
    row = lax.broadcasted_iota(jnp.int32, (count, count), 0)
    column = lax.broadcasted_iota(jnp.int32, (count, count), 1)
    earlier = jnp.where(row < column, 1.0, 0.0).astype(jnp.bfloat16)
    named = jnp.broadcast_to(hit, (16, count)).astype(jnp.bfloat16)
    slot = jnp.dot(named, earlier, preferred_element_type=jnp.float32)[:1].astype(jnp.int32)
    slot = jnp.where((hit > 0.0) & (slot < limits_ref[0, owner]), slot, -1)
    slot_ids = lax.broadcasted_iota(jnp.int32, (capacity, count), 0)
    select = jnp.where(slot_ids == slot, 1.0, 0.0).astype(jnp.bfloat16)
    select_ref[...] = select
    rows_ref[...] = jnp.dot(
        select, tokens_ref[...], preferred_element_type=jnp.float32
    ).astype(rows_ref.dtype)


def route(owner, limits, assignments, tokens, capacity):
    count, width = tokens.shape
    whole = pl.BlockSpec(memory_space=pltpu.VMEM)
    scalars = pl.BlockSpec(memory_space=pltpu.SMEM)
    return pl.pallas_call(
        route_kernel,
        in_specs=[scalars, scalars, whole, whole],
        out_specs=[whole, whole],
        out_shape=[
            jax.ShapeDtypeStruct((capacity, count), jnp.bfloat16),
            jax.ShapeDtypeStruct((capacity, width), jnp.bfloat16),
        ],
        compiler_params=pltpu.CompilerParams(vmem_limit_bytes=16 << 20),
        cost_estimate=pl.CostEstimate(
            flops=2 * capacity * count * width,
            bytes_accessed=2 * (count + capacity) * width,
            transcendentals=0,
        ),
        name="route",
    )(owner, limits, assignments, tokens)


def ffn_kernel(rows_hbm, gate_ref, up_ref, gate2_ref, up2_ref, out_ref, rows_ref, sems):
    chunks, _, chunk = rows_ref.shape
    copies = [
        pltpu.make_async_copy(
            rows_hbm.at[:, pl.ds(index * chunk, chunk)], rows_ref.at[index], sems.at[index]
        )
        for index in range(chunks)
    ]
    for copy in copies:
        copy.start()
    units = gate_ref.shape[1]
    totals = [None, None]
    for index in range(chunks):
        copies[index].wait()
        rows = rows_ref[index]
        part = pl.ds(index * chunk, chunk)
        for side, (gate, up) in enumerate(((gate_ref, up_ref), (gate2_ref, up2_ref))):
            both = jnp.concatenate([gate[part, :], up[part, :]], axis=1)
            product = jnp.dot(rows, both, preferred_element_type=jnp.float32)
            totals[side] = product if index == 0 else totals[side] + product
    for side, total in enumerate(totals):
        gate = total[:, :units]
        hidden = gate / (1.0 + jnp.exp(-gate)) * total[:, units:]
        out_ref[:, side * units : (side + 1) * units] = hidden.astype(out_ref.dtype)


def ffn(rows, gate, up, gate2, up2, chunk=1024):
    count, width = rows.shape
    units = gate.shape[1]
    whole = pl.BlockSpec(memory_space=pltpu.VMEM)
    return pl.pallas_call(
        ffn_kernel,
        in_specs=[pl.BlockSpec(memory_space=pltpu.HBM)] + [whole] * 4,
        out_specs=whole,
        out_shape=jax.ShapeDtypeStruct((count, 2 * units), jnp.bfloat16),
        scratch_shapes=[
            pltpu.VMEM((width // chunk, count, chunk), jnp.bfloat16),
            pltpu.SemaphoreType.DMA((width // chunk,)),
        ],
        compiler_params=pltpu.CompilerParams(vmem_limit_bytes=32 << 20),
        cost_estimate=pl.CostEstimate(
            flops=8 * count * width * units,
            bytes_accessed=2 * count * width + 8 * width * units,
            transcendentals=2 * count * units,
        ),
        name="ffn",
    )(rows, gate, up, gate2, up2)


def down_kernel(hidden_ref, down_ref, down2_ref, out_ref):
    parts = hidden_ref.shape[0]
    units = down_ref.shape[0] // parts
    total = None
    for index in range(parts):
        part = pl.ds(index * units, units)
        both = jnp.concatenate([down_ref[part, :], down2_ref[part, :]], axis=0)
        product = jnp.dot(hidden_ref[index], both, preferred_element_type=jnp.float32)
        total = product if index == 0 else total + product
    out_ref[...] = total.astype(out_ref.dtype)


def down(hidden, weight, weight2):
    parts, count, units = hidden.shape
    columns = weight.shape[1]
    return pl.pallas_call(
        down_kernel,
        out_shape=jax.ShapeDtypeStruct((count, columns), jnp.bfloat16),
        compiler_params=pltpu.CompilerParams(vmem_limit_bytes=24 << 20),
        cost_estimate=pl.CostEstimate(
            flops=2 * parts * count * units * columns,
            bytes_accessed=2 * parts * units * (count + columns) + 2 * count * columns,
            transcendentals=0,
        ),
        name="down",
    )(hidden, weight, weight2)


def weigh_kernel(parts_ref, select_ref, gate_ref, out_ref):
    select = select_ref[...]
    total = jnp.sum(parts_ref[...].astype(jnp.float32), axis=0).astype(jnp.bfloat16)
    gate = jnp.sum(select.astype(jnp.float32) * gate_ref[...], axis=1, keepdims=True)
    weighted = (total.astype(jnp.float32) * gate).astype(jnp.bfloat16)
    out_ref[...] = lax.dot_general(
        select, weighted, (((0,), (0,)), ((), ())), preferred_element_type=jnp.float32
    ).astype(out_ref.dtype)


def weigh(parts, select, gate):
    count = select.shape[1]
    columns = parts.shape[2]
    return pl.pallas_call(
        weigh_kernel,
        out_shape=jax.ShapeDtypeStruct((count, columns), jnp.bfloat16),
        compiler_params=pltpu.CompilerParams(vmem_limit_bytes=24 << 20),
        cost_estimate=pl.CostEstimate(
            flops=2 * count * select.shape[0] * columns,
            bytes_accessed=2 * parts.size + 2 * count * columns,
            transcendentals=0,
        ),
        name="weigh",
    )(parts, select, gate)


def local(tokens, router_weight, gate_weight, up_weight, down_weight, assignments, limits):
    local_rows = tokens.shape[0]
    experts = router_weight.shape[1]
    rings = lax.axis_size("y")
    shards = rings * CORES
    owners = lax.axis_size("exp")
    capacity = min(local_rows, max(2, 3 * local_rows * TOP // (2 * experts)))
    out_rows = local_rows // owners
    target = local_rows * shards * TOP / experts
    owner = lax.axis_index("exp")

    select, expert_rows = route(
        jnp.reshape(owner, (1,)).astype(jnp.int32), limits, assignments.T, tokens, capacity
    )
    rows = lax.all_gather(expert_rows, "y", axis=0, tiled=True)

    w_gate, w_up, w_down, tokens2, _ = lax.optimization_barrier(
        (gate_weight[0], up_weight[0], down_weight[0], tokens, expert_rows)
    )
    gate2, up2, down2 = swap_cores(w_gate), swap_cores(w_up), swap_cores(w_down)

    logits = lax.dot_general(
        router_weight, tokens2, (((0,), (1,)), ((), ())), preferred_element_type=jnp.float32
    )
    capped = SOFT_CAP * jnp.tanh(logits / SOFT_CAP)
    scores = lax.all_gather(capped, ("y", "core"), axis=0)
    weights = jnp.exp(scores)
    weights = weights * (TOP / jnp.sum(weights, axis=1, keepdims=True))
    for repeat in range(ITERS):
        weights = weights * (target / jnp.sum(weights, axis=(0, 2), keepdims=True))
        weights = weights * (TOP / jnp.sum(weights, axis=1, keepdims=True))
    shard = lax.axis_index("y") * CORES + lax.axis_index("core")
    own = lax.dynamic_slice(weights, (shard, owner, 0), (1, 1, local_rows))[0]

    hidden = ffn(rows, w_gate, w_up, gate2, up2)
    full_hidden = lax.all_gather(hidden, "tp", axis=0)
    partial = down(full_hidden, w_down, down2)
    parts = lax.all_to_all(partial.reshape(rings, capacity, partial.shape[1]), "y", 0, 0)
    shares = weigh(parts, select, own)
    shares = lax.all_to_all(shares.reshape(owners, out_rows, shares.shape[1]), "exp", 0, 0)
    return jnp.sum(shares.astype(jnp.float32), axis=0).astype(jnp.bfloat16)


def solution(mesh):
    shape = mesh.devices.shape
    fine = Mesh(
        mesh.devices.reshape((shape[0] // CORES, CORES) + shape[1:]), ("y", "core", "exp", "tp")
    )
    tok = ("y", "core")
    placed = (
        P(tok, None),
        P(),
        P("exp", None, tok + ("tp",)),
        P("exp", None, tok + ("tp",)),
        P("exp", tok, "tp"),
        P(tok, None),
        P(tok, None),
    )
    return jax.shard_map(
        local, mesh=fine, in_specs=placed, out_specs=P(tok + ("exp",), "tp"), check_vma=False
    )
```

```python
import jax
import jax.numpy as jnp
from jax import lax
from jax.experimental import pallas as pl
from jax.experimental.pallas import tpu as pltpu
from jax.sharding import Mesh, PartitionSpec as P

TOP = 2
ITERS = 4
SOFT_CAP = 8.0
CORES = 2
VMEM_BYTES = 64 << 20


def swap_cores(value):
    return lax.ppermute(value, "core", [(0, 1), (1, 0)])


def route_kernel(owner_ref, limits_ref, assign_ref, tokens_hbm, select_ref, rows_ref, tokens_ref, sems):
    width = tokens_ref.shape[1]
    chunks = sems.shape[0]
    parts = [pl.ds(index * (width // chunks), width // chunks) for index in range(chunks)]
    copies = [
        pltpu.make_async_copy(tokens_hbm.at[:, part], tokens_ref.at[:, part], sems.at[index])
        for index, part in enumerate(parts)
    ]
    for copy in copies:
        copy.start()
    owner = owner_ref[0]
    count = assign_ref.shape[1]
    capacity = select_ref.shape[0]
    hit = jnp.sum(jnp.where(assign_ref[...] == owner, 1.0, 0.0), axis=0, keepdims=True)
    row = lax.broadcasted_iota(jnp.int32, (count, count), 0)
    column = lax.broadcasted_iota(jnp.int32, (count, count), 1)
    earlier = jnp.where(row < column, 1.0, 0.0).astype(jnp.bfloat16)
    named = jnp.broadcast_to(hit, (16, count)).astype(jnp.bfloat16)
    slot = jnp.dot(named, earlier, preferred_element_type=jnp.float32)[:1].astype(jnp.int32)
    slot = jnp.where((hit > 0.0) & (slot < limits_ref[0, owner]), slot, -1)
    slot_ids = lax.broadcasted_iota(jnp.int32, (capacity, count), 0)
    select = jnp.where(slot_ids == slot, 1.0, 0.0).astype(jnp.bfloat16)
    select_ref[...] = select
    for copy, part in zip(copies, parts):
        copy.wait()
        rows_ref[:, part] = jnp.dot(
            select, tokens_ref[:, part], preferred_element_type=jnp.float32
        ).astype(rows_ref.dtype)


def route(owner, limits, assignments, tokens, capacity, chunks=4):
    count, width = tokens.shape
    whole = pl.BlockSpec(memory_space=pltpu.VMEM)
    scalars = pl.BlockSpec(memory_space=pltpu.SMEM)
    return pl.pallas_call(
        route_kernel,
        in_specs=[scalars, scalars, whole, pl.BlockSpec(memory_space=pltpu.HBM)],
        out_specs=[whole, whole],
        out_shape=[
            jax.ShapeDtypeStruct((capacity, count), jnp.bfloat16),
            jax.ShapeDtypeStruct((capacity, width), jnp.bfloat16),
        ],
        scratch_shapes=[
            pltpu.VMEM((count, width), jnp.bfloat16),
            pltpu.SemaphoreType.DMA((chunks,)),
        ],
        compiler_params=pltpu.CompilerParams(vmem_limit_bytes=VMEM_BYTES),
        cost_estimate=pl.CostEstimate(
            flops=2 * capacity * count * width,
            bytes_accessed=2 * (count + capacity) * width,
            transcendentals=0,
        ),
        name="route",
    )(owner, limits, assignments, tokens)


def ffn_kernel(rows_hbm, gate_hbm, up_hbm, gate2_hbm, up2_hbm, out_ref, rows_ref, weight_ref, sems):
    chunks, chunk, width = weight_ref.shape
    units = width // 4
    copies = []
    for index in range(chunks):
        part = pl.ds(index * chunk, chunk)
        ends = [(rows_hbm.at[:, part], rows_ref.at[index])]
        for place, ref in enumerate((gate_hbm, up_hbm, gate2_hbm, up2_hbm)):
            ends.append(
                (ref.at[part, :], weight_ref.at[index, :, pl.ds(place * units, units)])
            )
        copies.append(
            [
                pltpu.make_async_copy(source, sink, sems.at[index, place])
                for place, (source, sink) in enumerate(ends)
            ]
        )
    for group in copies:
        for copy in group:
            copy.start()
    total = None
    for index, group in enumerate(copies):
        for copy in group:
            copy.wait()
        product = jnp.dot(
            rows_ref[index], weight_ref[index], preferred_element_type=jnp.float32
        )
        total = product if index == 0 else total + product
    for side in range(2):
        gate = total[:, 2 * side * units : (2 * side + 1) * units]
        up = total[:, (2 * side + 1) * units : (2 * side + 2) * units]
        hidden = gate / (1.0 + jnp.exp(-gate)) * up
        out_ref[:, side * units : (side + 1) * units] = hidden.astype(out_ref.dtype)


def ffn(rows, gate, up, gate2, up2, chunk=1024):
    count, width = rows.shape
    units = gate.shape[1]
    chunks = width // chunk
    return pl.pallas_call(
        ffn_kernel,
        in_specs=[pl.BlockSpec(memory_space=pltpu.HBM)] * 5,
        out_specs=pl.BlockSpec(memory_space=pltpu.VMEM),
        out_shape=jax.ShapeDtypeStruct((count, 2 * units), jnp.bfloat16),
        scratch_shapes=[
            pltpu.VMEM((chunks, count, chunk), jnp.bfloat16),
            pltpu.VMEM((chunks, chunk, 4 * units), jnp.bfloat16),
            pltpu.SemaphoreType.DMA((chunks, 5)),
        ],
        compiler_params=pltpu.CompilerParams(vmem_limit_bytes=VMEM_BYTES),
        cost_estimate=pl.CostEstimate(
            flops=8 * count * width * units,
            bytes_accessed=2 * count * width + 8 * width * units,
            transcendentals=2 * count * units,
        ),
        name="ffn",
    )(rows, gate, up, gate2, up2)


def down_kernel(hidden_hbm, down_hbm, down2_hbm, out_ref, hidden_ref, weight_ref, sems):
    parts, count, units = hidden_ref.shape
    half = units // 2
    copies = []
    for index in range(parts):
        part = pl.ds(index * half, half)
        ends = (
            (hidden_hbm.at[index], hidden_ref.at[index]),
            (down_hbm.at[part, :], weight_ref.at[index, pl.ds(0, half), :]),
            (down2_hbm.at[part, :], weight_ref.at[index, pl.ds(half, half), :]),
        )
        copies.append(
            [
                pltpu.make_async_copy(source, sink, sems.at[index, place])
                for place, (source, sink) in enumerate(ends)
            ]
        )
    for group in copies:
        for copy in group:
            copy.start()
    total = None
    for index, group in enumerate(copies):
        for copy in group:
            copy.wait()
        product = jnp.dot(
            hidden_ref[index], weight_ref[index], preferred_element_type=jnp.float32
        )
        total = product if index == 0 else total + product
    out_ref[...] = total.astype(out_ref.dtype)


def down(hidden, weight, weight2):
    parts, count, units = hidden.shape
    columns = weight.shape[1]
    return pl.pallas_call(
        down_kernel,
        in_specs=[pl.BlockSpec(memory_space=pltpu.HBM)] * 3,
        out_specs=pl.BlockSpec(memory_space=pltpu.VMEM),
        out_shape=jax.ShapeDtypeStruct((count, columns), jnp.bfloat16),
        scratch_shapes=[
            pltpu.VMEM((parts, count, units), jnp.bfloat16),
            pltpu.VMEM((parts, units, columns), jnp.bfloat16),
            pltpu.SemaphoreType.DMA((parts, 3)),
        ],
        compiler_params=pltpu.CompilerParams(vmem_limit_bytes=VMEM_BYTES),
        cost_estimate=pl.CostEstimate(
            flops=2 * parts * count * units * columns,
            bytes_accessed=2 * parts * units * (count + columns) + 2 * count * columns,
            transcendentals=0,
        ),
        name="down",
    )(hidden, weight, weight2)


def weigh_kernel(parts_ref, select_ref, gate_ref, out_ref):
    select = select_ref[...]
    total = jnp.sum(parts_ref[...].astype(jnp.float32), axis=0).astype(jnp.bfloat16)
    gate = jnp.sum(select.astype(jnp.float32) * gate_ref[...], axis=1, keepdims=True)
    weighted = (total.astype(jnp.float32) * gate).astype(jnp.bfloat16)
    out_ref[...] = lax.dot_general(
        select, weighted, (((0,), (0,)), ((), ())), preferred_element_type=jnp.float32
    ).astype(out_ref.dtype)


def weigh(parts, select, gate):
    count = select.shape[1]
    columns = parts.shape[2]
    return pl.pallas_call(
        weigh_kernel,
        out_shape=jax.ShapeDtypeStruct((count, columns), jnp.bfloat16),
        compiler_params=pltpu.CompilerParams(vmem_limit_bytes=VMEM_BYTES),
        cost_estimate=pl.CostEstimate(
            flops=2 * count * select.shape[0] * columns,
            bytes_accessed=2 * parts.size + 2 * count * columns,
            transcendentals=0,
        ),
        name="weigh",
    )(parts, select, gate)


def local(tokens, router_weight, gate_weight, up_weight, down_weight, assignments, limits):
    local_rows = tokens.shape[0]
    experts = router_weight.shape[1]
    rings = lax.axis_size("y")
    shards = rings * CORES
    owners = lax.axis_size("exp")
    capacity = min(local_rows, max(2, 3 * local_rows * TOP // (2 * experts)))
    out_rows = local_rows // owners
    target = local_rows * shards * TOP / experts
    owner = lax.axis_index("exp")

    select, expert_rows = route(
        jnp.reshape(owner, (1,)).astype(jnp.int32), limits, assignments.T, tokens, capacity
    )
    rows = lax.all_gather(expert_rows, "y", axis=0, tiled=True)

    w_gate, w_up, w_down, tokens2, _ = lax.optimization_barrier(
        (gate_weight[0], up_weight[0], down_weight[0], tokens, expert_rows)
    )
    gate2, up2, down2 = swap_cores(w_gate), swap_cores(w_up), swap_cores(w_down)

    logits = lax.dot_general(
        router_weight, tokens2, (((0,), (1,)), ((), ())), preferred_element_type=jnp.float32
    )
    capped = SOFT_CAP * jnp.tanh(logits / SOFT_CAP)
    hidden = ffn(rows, w_gate, w_up, gate2, up2)
    full_hidden = lax.all_gather(hidden, "tp", axis=0)
    partial = down(full_hidden, w_down, down2)
    capped, partial = lax.optimization_barrier((capped, partial))
    parts = lax.all_to_all(partial.reshape(rings, capacity, partial.shape[1]), "y", 0, 0)
    scores = lax.all_gather(capped, ("y", "core"), axis=0)
    weights = jnp.exp(scores)
    weights = weights * (TOP / jnp.sum(weights, axis=1, keepdims=True))
    for repeat in range(ITERS):
        weights = weights * (target / jnp.sum(weights, axis=(0, 2), keepdims=True))
        weights = weights * (TOP / jnp.sum(weights, axis=1, keepdims=True))
    shard = lax.axis_index("y") * CORES + lax.axis_index("core")
    own = lax.dynamic_slice(weights, (shard, owner, 0), (1, 1, local_rows))[0]

    shares = weigh(parts, select, own)
    shares = lax.all_to_all(shares.reshape(owners, out_rows, shares.shape[1]), "exp", 0, 0)
    return jnp.sum(shares.astype(jnp.float32), axis=0).astype(jnp.bfloat16)


def solution(mesh):
    shape = mesh.devices.shape
    fine = Mesh(
        mesh.devices.reshape((shape[0] // CORES, CORES) + shape[1:]), ("y", "core", "exp", "tp")
    )
    tok = ("y", "core")
    placed = (
        P(tok, None),
        P(),
        P("exp", None, tok + ("tp",)),
        P("exp", None, tok + ("tp",)),
        P("exp", tok, "tp"),
        P(tok, None),
        P(tok, None),
    )
    return jax.shard_map(
        local, mesh=fine, in_specs=placed, out_specs=P(tok + ("exp",), "tp"), check_vma=False
    )
```

```python
import jax
import jax.numpy as jnp
from jax import lax
from jax.experimental import pallas as pl
from jax.experimental.pallas import tpu as pltpu
from jax.sharding import Mesh, PartitionSpec as P

TOP = 2
ITERS = 4
SOFT_CAP = 8.0
CORES = 2
ALL_VMEM = 64 << 20


def swap_cores(value):
    return lax.ppermute(value, "core", [(0, 1), (1, 0)])


def route_kernel(
    owner_ref, limits_hbm, assign_hbm, tokens_hbm, select_ref, rows_hbm,
    limits_ref, assign_ref, tokens_ref, rows_ref, sems, out_sems
):
    width = tokens_ref.shape[1]
    chunks = out_sems.shape[0]
    parts = [pl.ds(index * (width // chunks), width // chunks) for index in range(chunks)]
    small = [
        pltpu.make_async_copy(limits_hbm, limits_ref, sems.at[chunks]),
        pltpu.make_async_copy(assign_hbm, assign_ref, sems.at[chunks + 1]),
    ]
    copies = [
        pltpu.make_async_copy(tokens_hbm.at[:, part], tokens_ref.at[:, part], sems.at[index])
        for index, part in enumerate(parts)
    ]
    for copy in small + copies:
        copy.start()
    owner = owner_ref[0]
    capacity, count = select_ref.shape
    row = lax.broadcasted_iota(jnp.int32, (count, count), 0)
    column = lax.broadcasted_iota(jnp.int32, (count, count), 1)
    earlier = jnp.where(row < column, 1.0, 0.0).astype(jnp.bfloat16)
    slot_ids = lax.broadcasted_iota(jnp.int32, (capacity, count), 0)
    for copy in small:
        copy.wait()
    hit = jnp.sum(jnp.where(assign_ref[...] == owner, 1.0, 0.0), axis=0, keepdims=True)
    named = jnp.broadcast_to(hit, (16, count)).astype(jnp.bfloat16)
    slot = jnp.dot(named, earlier, preferred_element_type=jnp.float32)[:1].astype(jnp.int32)
    slot = jnp.where((hit > 0.0) & (slot < limits_ref[0, owner]), slot, -1)
    select = jnp.where(slot_ids == slot, 1.0, 0.0).astype(jnp.bfloat16)
    select_ref[...] = select
    outs = []
    for index, part in enumerate(parts):
        copies[index].wait()
        rows_ref[:, part] = jnp.dot(
            select, tokens_ref[:, part], preferred_element_type=jnp.float32
        ).astype(rows_ref.dtype)
        outs.append(
            pltpu.make_async_copy(
                rows_ref.at[:, part], rows_hbm.at[:, part], out_sems.at[index]
            )
        )
        outs[-1].start()
    for copy in outs:
        copy.wait()


def route(owner, limits, assignments, tokens, capacity, chunks=4):
    count, width = tokens.shape
    far = pl.BlockSpec(memory_space=pltpu.HBM)
    return pl.pallas_call(
        route_kernel,
        in_specs=[pl.BlockSpec(memory_space=pltpu.SMEM), far, far, far],
        out_specs=[pl.BlockSpec(memory_space=pltpu.VMEM), far],
        out_shape=[
            jax.ShapeDtypeStruct((capacity, count), jnp.bfloat16),
            jax.ShapeDtypeStruct((capacity, width), jnp.bfloat16),
        ],
        scratch_shapes=[
            pltpu.SMEM(limits.shape, jnp.int32),
            pltpu.VMEM(assignments.shape, jnp.int32),
            pltpu.VMEM((count, width), jnp.bfloat16),
            pltpu.VMEM((capacity, width), jnp.bfloat16),
            pltpu.SemaphoreType.DMA((chunks + 2,)),
            pltpu.SemaphoreType.DMA((chunks,)),
        ],
        compiler_params=pltpu.CompilerParams(vmem_limit_bytes=ALL_VMEM),
        cost_estimate=pl.CostEstimate(
            flops=2 * capacity * count * width,
            bytes_accessed=2 * (count + capacity) * width,
            transcendentals=0,
        ),
        name="route",
    )(owner, limits, assignments, tokens)


def ffn_kernel(rows_hbm, gate_hbm, up_hbm, gate2_hbm, up2_hbm, out_ref, rows_ref, weight_ref, sems):
    chunks, chunk, width = weight_ref.shape
    units = width // 4
    copies = []
    for index in range(chunks):
        part = pl.ds(index * chunk, chunk)
        ends = [(rows_hbm.at[:, part], rows_ref.at[index])]
        for place, ref in enumerate((gate_hbm, up_hbm, gate2_hbm, up2_hbm)):
            ends.append(
                (ref.at[part, :], weight_ref.at[index, :, pl.ds(place * units, units)])
            )
        copies.append(
            [
                pltpu.make_async_copy(source, sink, sems.at[index, place])
                for place, (source, sink) in enumerate(ends)
            ]
        )
    for group in copies:
        for copy in group:
            copy.start()
    total = None
    for index, group in enumerate(copies):
        for copy in group:
            copy.wait()
        product = jnp.dot(
            rows_ref[index], weight_ref[index], preferred_element_type=jnp.float32
        )
        total = product if index == 0 else total + product
    for side in range(2):
        gate = total[:, 2 * side * units : (2 * side + 1) * units]
        up = total[:, (2 * side + 1) * units : (2 * side + 2) * units]
        hidden = gate / (1.0 + jnp.exp(-gate)) * up
        out_ref[:, side * units : (side + 1) * units] = hidden.astype(out_ref.dtype)


def ffn(rows, gate, up, gate2, up2, chunk=512):
    count, width = rows.shape
    units = gate.shape[1]
    chunks = width // chunk
    return pl.pallas_call(
        ffn_kernel,
        in_specs=[pl.BlockSpec(memory_space=pltpu.HBM)] * 5,
        out_specs=pl.BlockSpec(memory_space=pltpu.VMEM),
        out_shape=jax.ShapeDtypeStruct((count, 2 * units), jnp.bfloat16),
        scratch_shapes=[
            pltpu.VMEM((chunks, count, chunk), jnp.bfloat16),
            pltpu.VMEM((chunks, chunk, 4 * units), jnp.bfloat16),
            pltpu.SemaphoreType.DMA((chunks, 5)),
        ],
        compiler_params=pltpu.CompilerParams(vmem_limit_bytes=ALL_VMEM),
        cost_estimate=pl.CostEstimate(
            flops=8 * count * width * units,
            bytes_accessed=2 * count * width + 8 * width * units,
            transcendentals=2 * count * units,
        ),
        name="ffn",
    )(rows, gate, up, gate2, up2)


def down_kernel(hidden_ref, down_ref, down2_ref, out_ref):
    parts = hidden_ref.shape[0]
    units = down_ref.shape[0] // parts
    total = None
    for index in range(parts):
        part = pl.ds(index * units, units)
        both = jnp.concatenate([down_ref[part, :], down2_ref[part, :]], axis=0)
        product = jnp.dot(hidden_ref[index], both, preferred_element_type=jnp.float32)
        total = product if index == 0 else total + product
    out_ref[...] = total.astype(out_ref.dtype)


def down(hidden, weight, weight2):
    parts, count, units = hidden.shape
    columns = weight.shape[1]
    return pl.pallas_call(
        down_kernel,
        out_shape=jax.ShapeDtypeStruct((count, columns), jnp.bfloat16),
        compiler_params=pltpu.CompilerParams(vmem_limit_bytes=24 << 20),
        cost_estimate=pl.CostEstimate(
            flops=2 * parts * count * units * columns,
            bytes_accessed=2 * parts * units * (count + columns) + 2 * count * columns,
            transcendentals=0,
        ),
        name="down",
    )(hidden, weight, weight2)


def weigh_kernel(parts_ref, select_ref, gate_ref, out_ref):
    select = select_ref[...]
    total = jnp.sum(parts_ref[...].astype(jnp.float32), axis=0).astype(jnp.bfloat16)
    gate = jnp.sum(select.astype(jnp.float32) * gate_ref[...], axis=1, keepdims=True)
    weighted = (total.astype(jnp.float32) * gate).astype(jnp.bfloat16)
    out_ref[...] = lax.dot_general(
        select, weighted, (((0,), (0,)), ((), ())), preferred_element_type=jnp.float32
    ).astype(out_ref.dtype)


def weigh(parts, select, gate):
    count = select.shape[1]
    columns = parts.shape[2]
    return pl.pallas_call(
        weigh_kernel,
        out_shape=jax.ShapeDtypeStruct((count, columns), jnp.bfloat16),
        compiler_params=pltpu.CompilerParams(vmem_limit_bytes=24 << 20),
        cost_estimate=pl.CostEstimate(
            flops=2 * count * select.shape[0] * columns,
            bytes_accessed=2 * parts.size + 2 * count * columns,
            transcendentals=0,
        ),
        name="weigh",
    )(parts, select, gate)


def local(tokens, router_weight, gate_weight, up_weight, down_weight, assignments, limits):
    local_rows = tokens.shape[0]
    experts = router_weight.shape[1]
    rings = lax.axis_size("y")
    shards = rings * CORES
    owners = lax.axis_size("exp")
    capacity = min(local_rows, max(2, 3 * local_rows * TOP // (2 * experts)))
    out_rows = local_rows // owners
    target = local_rows * shards * TOP / experts
    owner = lax.axis_index("exp")

    select, expert_rows = route(
        jnp.reshape(owner, (1,)).astype(jnp.int32), limits, assignments.T, tokens, capacity
    )
    rows = lax.all_gather(expert_rows, "y", axis=0, tiled=True)

    w_gate, w_up, w_down, tokens2, _ = lax.optimization_barrier(
        (gate_weight[0], up_weight[0], down_weight[0], tokens, expert_rows)
    )
    gate2, up2, down2 = swap_cores(w_gate), swap_cores(w_up), swap_cores(w_down)

    logits = lax.dot_general(
        router_weight, tokens2, (((0,), (1,)), ((), ())), preferred_element_type=jnp.float32
    )
    capped = SOFT_CAP * jnp.tanh(logits / SOFT_CAP)
    scores = lax.all_gather(capped, ("y", "core"), axis=0)
    weights = jnp.exp(scores)
    weights = weights * (TOP / jnp.sum(weights, axis=1, keepdims=True))
    for repeat in range(ITERS):
        weights = weights * (target / jnp.sum(weights, axis=(0, 2), keepdims=True))
        weights = weights * (TOP / jnp.sum(weights, axis=1, keepdims=True))
    shard = lax.axis_index("y") * CORES + lax.axis_index("core")
    own = lax.dynamic_slice(weights, (shard, owner, 0), (1, 1, local_rows))[0]

    hidden = ffn(rows, w_gate, w_up, gate2, up2)
    full_hidden = lax.all_gather(hidden, "tp", axis=0)
    partial = down(full_hidden, w_down, down2)
    parts = lax.all_to_all(partial.reshape(rings, capacity, partial.shape[1]), "y", 0, 0)
    shares = weigh(parts, select, own)
    shares = lax.all_to_all(shares.reshape(owners, out_rows, shares.shape[1]), "exp", 0, 0)
    return jnp.sum(shares.astype(jnp.float32), axis=0).astype(jnp.bfloat16)


def solution(mesh):
    shape = mesh.devices.shape
    fine = Mesh(
        mesh.devices.reshape((shape[0] // CORES, CORES) + shape[1:]), ("y", "core", "exp", "tp")
    )
    tok = ("y", "core")
    placed = (
        P(tok, None),
        P(),
        P("exp", None, tok + ("tp",)),
        P("exp", None, tok + ("tp",)),
        P("exp", tok, "tp"),
        P(tok, None),
        P(tok, None),
    )
    return jax.shard_map(
        local, mesh=fine, in_specs=placed, out_specs=P(tok + ("exp",), "tp"), check_vma=False
    )
```

```python
import jax
import jax.numpy as jnp
from jax import lax
from jax.experimental import pallas as pl
from jax.experimental.pallas import tpu as pltpu
from jax.sharding import Mesh, PartitionSpec as P

TOP = 2
ITERS = 4
SOFT_CAP = 8.0
CORES = 2
ALL_VMEM = 64 << 20
FFN_VMEM = 60 << 20
DIRECT = 512
LANES = 128


def swap_cores(value):
    return lax.ppermute(value, "core", [(0, 1), (1, 0)])


def route_kernel(
    ids_ref, limits_hbm, assign_hbm, tokens_hbm, select_ref, direct_ref, spread_hbm,
    limits_ref, assign_ref, near_ref, far_ref, own_ref, sems, out_sems
):
    direct = near_ref.shape[1]
    share = far_ref.shape[1]
    owner = ids_ref[0]
    first = pl.multiple_of(direct + ids_ref[1] * share, 128)
    copies = [
        pltpu.make_async_copy(source, sink, sems.at[index])
        for index, (source, sink) in enumerate(
            (
                (limits_hbm, limits_ref),
                (assign_hbm, assign_ref),
                (tokens_hbm.at[:, pl.ds(first, share)], far_ref),
                (tokens_hbm.at[:, pl.ds(0, direct)], near_ref),
            )
        )
    ]
    for copy in copies:
        copy.start()
    capacity, count = select_ref.shape
    row = lax.broadcasted_iota(jnp.int32, (count, count), 0)
    column = lax.broadcasted_iota(jnp.int32, (count, count), 1)
    earlier = jnp.where(row < column, 1.0, 0.0).astype(jnp.bfloat16)
    slot_ids = lax.broadcasted_iota(jnp.int32, (capacity, count), 0)
    copies[0].wait()
    copies[1].wait()
    hit = jnp.sum(jnp.where(assign_ref[...] == owner, 1.0, 0.0), axis=0, keepdims=True)
    named = jnp.broadcast_to(hit, (16, count)).astype(jnp.bfloat16)
    slot = jnp.dot(named, earlier, preferred_element_type=jnp.float32)[:1].astype(jnp.int32)
    slot = jnp.where((hit > 0.0) & (slot < limits_ref[0, owner]), slot, -1)
    select = jnp.where(slot_ids == slot, 1.0, 0.0).astype(jnp.bfloat16)
    select_ref[...] = select
    copies[2].wait()
    own_ref[...] = jnp.dot(
        select, far_ref[...], preferred_element_type=jnp.float32
    ).astype(own_ref.dtype)
    outs = [
        pltpu.make_async_copy(own_ref, spread_hbm.at[index], out_sems.at[index])
        for index in range(spread_hbm.shape[0])
    ]
    for copy in outs:
        copy.start()
    copies[3].wait()
    direct_ref[...] = jnp.dot(
        select, near_ref[...], preferred_element_type=jnp.float32
    ).astype(direct_ref.dtype)
    for copy in outs:
        copy.wait()


def route(ids, limits, assignments, tokens, capacity, direct, share, rings):
    count = tokens.shape[0]
    far = pl.BlockSpec(memory_space=pltpu.HBM)
    near = pl.BlockSpec(memory_space=pltpu.VMEM)
    return pl.pallas_call(
        route_kernel,
        in_specs=[pl.BlockSpec(memory_space=pltpu.SMEM), far, far, far],
        out_specs=[near, near, far],
        out_shape=[
            jax.ShapeDtypeStruct((capacity, count), jnp.bfloat16),
            jax.ShapeDtypeStruct((capacity, direct), jnp.bfloat16),
            jax.ShapeDtypeStruct((rings, capacity, share), jnp.bfloat16),
        ],
        scratch_shapes=[
            pltpu.SMEM(limits.shape, jnp.int32),
            pltpu.VMEM(assignments.shape, jnp.int32),
            pltpu.VMEM((count, direct), jnp.bfloat16),
            pltpu.VMEM((count, share), jnp.bfloat16),
            pltpu.VMEM((capacity, share), jnp.bfloat16),
            pltpu.SemaphoreType.DMA((4,)),
            pltpu.SemaphoreType.DMA((rings,)),
        ],
        compiler_params=pltpu.CompilerParams(vmem_limit_bytes=ALL_VMEM),
        cost_estimate=pl.CostEstimate(
            flops=2 * capacity * count * (direct + share),
            bytes_accessed=2 * (count + capacity) * (direct + share),
            transcendentals=0,
        ),
        name="route",
    )(ids, limits, assignments, tokens)


def ffn_kernel(
    near_hbm, far_hbm, gate_hbm, up_hbm, gate2_hbm, up2_hbm, out_ref,
    near_ref, far_ref, weight_ref, sems
):
    rings, capacity, direct = near_ref.shape
    shares, _, share = far_ref.shape
    width, columns = weight_ref.shape
    units = columns // 4
    copies = []
    for index in range(shares + 1):
        first, size = (0, direct) if index == 0 else (direct + (index - 1) * share, share)
        part = pl.ds(first, size)
        if index == 0:
            ends = [(near_hbm.at[:, pl.ds(0, capacity), :], near_ref)]
        else:
            ends = [(far_hbm.at[index - 1], far_ref.at[index - 1])]
        for place, ref in enumerate((gate_hbm, up_hbm, gate2_hbm, up2_hbm)):
            ends.append((ref.at[part, :], weight_ref.at[part, pl.ds(place * units, units)]))
        copies.append(
            [
                pltpu.make_async_copy(source, sink, sems.at[index, place])
                for place, (source, sink) in enumerate(ends)
            ]
        )
    for group in copies:
        for copy in group:
            copy.start()
    total = None
    for index, group in enumerate(copies):
        for copy in group:
            copy.wait()
        if index == 0:
            rows = near_ref[...].reshape(rings * capacity, direct)
            part = pl.ds(0, direct)
        else:
            rows = far_ref[index - 1]
            part = pl.ds(direct + (index - 1) * share, share)
        product = jnp.dot(rows, weight_ref[part, :], preferred_element_type=jnp.float32)
        total = product if index == 0 else total + product
    for side in range(2):
        gate = total[:, 2 * side * units : (2 * side + 1) * units]
        up = total[:, (2 * side + 1) * units : (2 * side + 2) * units]
        hidden = gate / (1.0 + jnp.exp(-gate)) * up
        out_ref[:, side * units : (side + 1) * units] = hidden.astype(out_ref.dtype)


def ffn(near, far, gate, up, gate2, up2, capacity):
    rings, _, direct = near.shape
    shares, count, share = far.shape
    width, units = gate.shape
    return pl.pallas_call(
        ffn_kernel,
        in_specs=[pl.BlockSpec(memory_space=pltpu.HBM)] * 6,
        out_specs=pl.BlockSpec(memory_space=pltpu.VMEM),
        out_shape=jax.ShapeDtypeStruct((count, 2 * units), jnp.bfloat16),
        scratch_shapes=[
            pltpu.VMEM((rings, capacity, direct), jnp.bfloat16),
            pltpu.VMEM((shares, count, share), jnp.bfloat16),
            pltpu.VMEM((width, 4 * units), jnp.bfloat16),
            pltpu.SemaphoreType.DMA((shares + 1, 5)),
        ],
        compiler_params=pltpu.CompilerParams(vmem_limit_bytes=FFN_VMEM),
        cost_estimate=pl.CostEstimate(
            flops=8 * count * width * units,
            bytes_accessed=2 * count * width + 8 * width * units,
            transcendentals=2 * count * units,
        ),
        name="ffn",
    )(near, far, gate, up, gate2, up2)


def down_kernel(hidden_ref, down_ref, down2_ref, out_ref):
    parts = hidden_ref.shape[0]
    units = down_ref.shape[0] // parts
    total = None
    for index in range(parts):
        part = pl.ds(index * units, units)
        both = jnp.concatenate([down_ref[part, :], down2_ref[part, :]], axis=0)
        product = jnp.dot(hidden_ref[index], both, preferred_element_type=jnp.float32)
        total = product if index == 0 else total + product
    out_ref[...] = total.astype(out_ref.dtype)


def down(hidden, weight, weight2):
    parts, count, units = hidden.shape
    columns = weight.shape[1]
    return pl.pallas_call(
        down_kernel,
        out_shape=jax.ShapeDtypeStruct((count, columns), jnp.bfloat16),
        compiler_params=pltpu.CompilerParams(vmem_limit_bytes=24 << 20),
        cost_estimate=pl.CostEstimate(
            flops=2 * parts * count * units * columns,
            bytes_accessed=2 * parts * units * (count + columns) + 2 * count * columns,
            transcendentals=0,
        ),
        name="down",
    )(hidden, weight, weight2)


def weigh_kernel(parts_ref, select_ref, gate_ref, out_ref):
    select = select_ref[...]
    total = jnp.sum(parts_ref[...].astype(jnp.float32), axis=0).astype(jnp.bfloat16)
    gate = jnp.sum(select.astype(jnp.float32) * gate_ref[...], axis=1, keepdims=True)
    weighted = (total.astype(jnp.float32) * gate).astype(jnp.bfloat16)
    out_ref[...] = lax.dot_general(
        select, weighted, (((0,), (0,)), ((), ())), preferred_element_type=jnp.float32
    ).astype(out_ref.dtype)


def weigh(parts, select, gate):
    count = select.shape[1]
    columns = parts.shape[2]
    return pl.pallas_call(
        weigh_kernel,
        out_shape=jax.ShapeDtypeStruct((count, columns), jnp.bfloat16),
        compiler_params=pltpu.CompilerParams(vmem_limit_bytes=24 << 20),
        cost_estimate=pl.CostEstimate(
            flops=2 * count * select.shape[0] * columns,
            bytes_accessed=2 * parts.size + 2 * count * columns,
            transcendentals=0,
        ),
        name="weigh",
    )(parts, select, gate)


def local(tokens, router_weight, gate_weight, up_weight, down_weight, assignments, limits):
    local_rows, width = tokens.shape
    experts = router_weight.shape[1]
    rings = lax.axis_size("y")
    shards = rings * CORES
    owners = lax.axis_size("exp")
    parts = lax.axis_size("tp")
    capacity = min(local_rows, max(2, 3 * local_rows * TOP // (2 * experts)))
    out_rows = local_rows // owners
    target = local_rows * shards * TOP / experts
    owner = lax.axis_index("exp")
    share = (width - DIRECT) // parts

    ids = jnp.stack([owner, lax.axis_index("tp")]).astype(jnp.int32)
    select, direct, spread = route(
        ids, limits, assignments.T, tokens, capacity, DIRECT, share, rings
    )
    own_share = lax.all_to_all(spread, "y", 0, 0).reshape(1, rings * capacity, share)

    w_gate, w_up, w_down, tokens2, _ = lax.optimization_barrier(
        (gate_weight[0], up_weight[0], down_weight[0], tokens, spread)
    )
    gate2, up2, down2 = swap_cores(w_gate), swap_cores(w_up), swap_cores(w_down)
    logits = lax.dot_general(
        router_weight, tokens2, (((0,), (1,)), ((), ())), preferred_element_type=jnp.float32
    )
    scores = SOFT_CAP * jnp.tanh(logits / SOFT_CAP)
    pieces = []
    for piece in range(3):
        pieces.append(lax.reduce_precision(scores, exponent_bits=8, mantissa_bits=7))
        scores = scores - pieces[-1]
    pieces = jnp.concatenate(pieces, axis=0).astype(jnp.bfloat16)
    count = pieces.shape[0]
    tail_rows = 16
    slots = tail_rows * DIRECT // local_rows
    pieces = jnp.pad(pieces, ((0, slots - count), (0, 0))).reshape(tail_rows, DIRECT)
    payload = jnp.concatenate([direct, pieces], axis=0)

    copies = jnp.broadcast_to(own_share, (parts,) + own_share.shape[1:])
    copies, payload, gate2, up2, down2 = lax.optimization_barrier(
        (copies, payload, gate2, up2, down2)
    )
    far = lax.all_to_all(copies, "tp", 0, 0)
    near = lax.all_gather(payload, "y", axis=0)

    hidden = ffn(near, far, w_gate, w_up, gate2, up2, capacity)
    full_hidden = lax.all_gather(hidden, "tp", axis=0)
    partial = down(full_hidden, w_down, down2)
    near, partial = lax.optimization_barrier((near, partial))
    sums = lax.all_to_all(partial.reshape(rings, capacity, partial.shape[1]), "y", 0, 0)
    tail = near[:, capacity:].reshape(rings, slots, local_rows)[:, :count]
    tail = jnp.sum(tail.reshape(rings, 3, experts, local_rows).astype(jnp.float32), axis=1)
    weights = jnp.exp(jnp.concatenate([tail, swap_cores(tail)], axis=0))
    weights = weights * (TOP / jnp.sum(weights, axis=1, keepdims=True))
    for repeat in range(ITERS):
        weights = weights * (target / jnp.sum(weights, axis=(0, 2), keepdims=True))
        weights = weights * (TOP / jnp.sum(weights, axis=1, keepdims=True))
    own = lax.dynamic_slice(weights, (lax.axis_index("y"), owner, 0), (1, 1, local_rows))[0]

    shares = weigh(sums, select, own)
    shares = lax.all_to_all(shares.reshape(owners, out_rows, shares.shape[1]), "exp", 0, 0)
    return jnp.sum(shares.astype(jnp.float32), axis=0).astype(jnp.bfloat16)


def solution(mesh):
    shape = mesh.devices.shape
    fine = Mesh(
        mesh.devices.reshape((shape[0] // CORES, CORES) + shape[1:]), ("y", "core", "exp", "tp")
    )
    tok = ("y", "core")
    placed = (
        P(tok, None),
        P(),
        P("exp", None, tok + ("tp",)),
        P("exp", None, tok + ("tp",)),
        P("exp", tok, "tp"),
        P(tok, None),
        P(tok, None),
    )
    return jax.shard_map(
        local, mesh=fine, in_specs=placed, out_specs=P(tok + ("exp",), "tp"), check_vma=False
    )
```

```python
import jax
import jax.numpy as jnp
from jax import lax
from jax.experimental import pallas as pl
from jax.experimental.pallas import tpu as pltpu
from jax.sharding import Mesh, PartitionSpec as P

TOP = 2
ITERS = 4
SOFT_CAP = 8.0
CORES = 2
ALL_VMEM = 64 << 20
FFN_VMEM = 60 << 20
SHARE = 256
TAIL = 16


def swap_cores(value):
    return lax.ppermute(value, "core", [(0, 1), (1, 0)])


def route_kernel(
    owner_ref, part_ref, limits_hbm, assign_hbm, tokens_hbm, select_ref, rows_hbm, share_ref,
    limits_ref, assign_ref, tokens_ref, own_ref, rows_ref, sems, out_sems
):
    width = tokens_ref.shape[1]
    share = own_ref.shape[1]
    chunks = out_sems.shape[0]
    parts = [pl.ds(index * (width // chunks), width // chunks) for index in range(chunks)]
    owner = owner_ref[0]
    first = pl.multiple_of(width + part_ref[0] * share, 128)
    small = [
        pltpu.make_async_copy(limits_hbm, limits_ref, sems.at[chunks]),
        pltpu.make_async_copy(assign_hbm, assign_ref, sems.at[chunks + 1]),
    ]
    copies = [
        pltpu.make_async_copy(tokens_hbm.at[:, part], tokens_ref.at[:, part], sems.at[index])
        for index, part in enumerate(parts)
    ]
    last = pltpu.make_async_copy(
        tokens_hbm.at[:, pl.ds(first, share)], own_ref, sems.at[chunks + 2]
    )
    for copy in small + copies + [last]:
        copy.start()
    capacity, count = select_ref.shape
    row = lax.broadcasted_iota(jnp.int32, (count, count), 0)
    column = lax.broadcasted_iota(jnp.int32, (count, count), 1)
    earlier = jnp.where(row < column, 1.0, 0.0).astype(jnp.bfloat16)
    slot_ids = lax.broadcasted_iota(jnp.int32, (capacity, count), 0)
    for copy in small:
        copy.wait()
    hit = jnp.sum(jnp.where(assign_ref[...] == owner, 1.0, 0.0), axis=0, keepdims=True)
    named = jnp.broadcast_to(hit, (16, count)).astype(jnp.bfloat16)
    slot = jnp.dot(named, earlier, preferred_element_type=jnp.float32)[:1].astype(jnp.int32)
    slot = jnp.where((hit > 0.0) & (slot < limits_ref[0, owner]), slot, -1)
    select = jnp.where(slot_ids == slot, 1.0, 0.0).astype(jnp.bfloat16)
    select_ref[...] = select
    outs = []
    for index, part in enumerate(parts):
        copies[index].wait()
        rows_ref[:, part] = jnp.dot(
            select, tokens_ref[:, part], preferred_element_type=jnp.float32
        ).astype(rows_ref.dtype)
        outs.append(
            pltpu.make_async_copy(
                rows_ref.at[:, part], rows_hbm.at[:, part], out_sems.at[index]
            )
        )
        outs[-1].start()
    last.wait()
    share_ref[...] = jnp.dot(
        select, own_ref[...], preferred_element_type=jnp.float32
    ).astype(share_ref.dtype)
    for copy in outs:
        copy.wait()


def route(owner, part, limits, assignments, tokens, capacity, share, parts, chunks=3):
    count = tokens.shape[0]
    width = tokens.shape[1] - parts * share
    far = pl.BlockSpec(memory_space=pltpu.HBM)
    near = pl.BlockSpec(memory_space=pltpu.VMEM)
    return pl.pallas_call(
        route_kernel,
        in_specs=[pl.BlockSpec(memory_space=pltpu.SMEM)] * 2 + [far] * 3,
        out_specs=[near, far, near],
        out_shape=[
            jax.ShapeDtypeStruct((capacity, count), jnp.bfloat16),
            jax.ShapeDtypeStruct((capacity, width), jnp.bfloat16),
            jax.ShapeDtypeStruct((capacity, share), jnp.bfloat16),
        ],
        scratch_shapes=[
            pltpu.SMEM(limits.shape, jnp.int32),
            pltpu.VMEM(assignments.shape, jnp.int32),
            pltpu.VMEM((count, width), jnp.bfloat16),
            pltpu.VMEM((count, share), jnp.bfloat16),
            pltpu.VMEM((capacity, width), jnp.bfloat16),
            pltpu.SemaphoreType.DMA((chunks + 3,)),
            pltpu.SemaphoreType.DMA((chunks,)),
        ],
        compiler_params=pltpu.CompilerParams(vmem_limit_bytes=ALL_VMEM),
        cost_estimate=pl.CostEstimate(
            flops=2 * capacity * count * (width + share),
            bytes_accessed=2 * (count + capacity) * (width + share),
            transcendentals=0,
        ),
        name="route",
    )(owner, part, limits, assignments, tokens)


def ffn_kernel(
    rows_hbm, last_hbm, gate_hbm, up_hbm, gate2_hbm, up2_hbm, out_ref, rows_ref, weight_ref, sems
):
    chunks, chunk, columns = weight_ref.shape
    units = columns // 4
    share = last_hbm.shape[2]
    main = rows_hbm.shape[1] // chunk
    copies = []
    for index in range(chunks):
        part = pl.ds(index * chunk, chunk)
        if index < main:
            ends = [(rows_hbm.at[:, part], rows_ref.at[index])]
        else:
            ends = [
                (
                    last_hbm.at[(index - main) * (chunk // share) + place],
                    rows_ref.at[index, :, pl.ds(place * share, share)],
                )
                for place in range(chunk // share)
            ]
        for place, ref in enumerate((gate_hbm, up_hbm, gate2_hbm, up2_hbm)):
            ends.append(
                (ref.at[part, :], weight_ref.at[index, :, pl.ds(place * units, units)])
            )
        copies.append(
            [
                pltpu.make_async_copy(source, sink, sems.at[index, place])
                for place, (source, sink) in enumerate(ends)
            ]
        )
    for group in copies:
        for copy in group:
            copy.start()
    total = None
    for index, group in enumerate(copies):
        for copy in group:
            copy.wait()
        product = jnp.dot(
            rows_ref[index], weight_ref[index], preferred_element_type=jnp.float32
        )
        total = product if index == 0 else total + product
    for side in range(2):
        gate = total[:, 2 * side * units : (2 * side + 1) * units]
        up = total[:, (2 * side + 1) * units : (2 * side + 2) * units]
        hidden = gate / (1.0 + jnp.exp(-gate)) * up
        out_ref[:, side * units : (side + 1) * units] = hidden.astype(out_ref.dtype)


def ffn(rows, last, gate, up, gate2, up2, chunk=512):
    count = rows.shape[0]
    width, units = gate.shape
    chunks = width // chunk
    return pl.pallas_call(
        ffn_kernel,
        in_specs=[pl.BlockSpec(memory_space=pltpu.HBM)] * 6,
        out_specs=pl.BlockSpec(memory_space=pltpu.VMEM),
        out_shape=jax.ShapeDtypeStruct((count, 2 * units), jnp.bfloat16),
        scratch_shapes=[
            pltpu.VMEM((chunks, count, chunk), jnp.bfloat16),
            pltpu.VMEM((chunks, chunk, 4 * units), jnp.bfloat16),
            pltpu.SemaphoreType.DMA((chunks, 4 + chunk // last.shape[2])),
        ],
        compiler_params=pltpu.CompilerParams(vmem_limit_bytes=FFN_VMEM),
        cost_estimate=pl.CostEstimate(
            flops=8 * count * width * units,
            bytes_accessed=2 * count * width + 8 * width * units,
            transcendentals=2 * count * units,
        ),
        name="ffn",
    )(rows, last, gate, up, gate2, up2)


def down_kernel(hidden_ref, down_ref, down2_ref, out_ref):
    parts = hidden_ref.shape[0]
    units = down_ref.shape[0] // parts
    total = None
    for index in range(parts):
        part = pl.ds(index * units, units)
        both = jnp.concatenate([down_ref[part, :], down2_ref[part, :]], axis=0)
        product = jnp.dot(hidden_ref[index], both, preferred_element_type=jnp.float32)
        total = product if index == 0 else total + product
    out_ref[...] = total.astype(out_ref.dtype)


def down(hidden, weight, weight2):
    parts, count, units = hidden.shape
    columns = weight.shape[1]
    return pl.pallas_call(
        down_kernel,
        out_shape=jax.ShapeDtypeStruct((count, columns), jnp.bfloat16),
        compiler_params=pltpu.CompilerParams(vmem_limit_bytes=24 << 20),
        cost_estimate=pl.CostEstimate(
            flops=2 * parts * count * units * columns,
            bytes_accessed=2 * parts * units * (count + columns) + 2 * count * columns,
            transcendentals=0,
        ),
        name="down",
    )(hidden, weight, weight2)


def weigh_kernel(parts_ref, select_ref, gate_ref, out_ref):
    select = select_ref[...]
    total = jnp.sum(parts_ref[...].astype(jnp.float32), axis=0).astype(jnp.bfloat16)
    gate = jnp.sum(select.astype(jnp.float32) * gate_ref[...], axis=1, keepdims=True)
    weighted = (total.astype(jnp.float32) * gate).astype(jnp.bfloat16)
    out_ref[...] = lax.dot_general(
        select, weighted, (((0,), (0,)), ((), ())), preferred_element_type=jnp.float32
    ).astype(out_ref.dtype)


def weigh(parts, select, gate):
    count = select.shape[1]
    columns = parts.shape[2]
    return pl.pallas_call(
        weigh_kernel,
        out_shape=jax.ShapeDtypeStruct((count, columns), jnp.bfloat16),
        compiler_params=pltpu.CompilerParams(vmem_limit_bytes=24 << 20),
        cost_estimate=pl.CostEstimate(
            flops=2 * count * select.shape[0] * columns,
            bytes_accessed=2 * parts.size + 2 * count * columns,
            transcendentals=0,
        ),
        name="weigh",
    )(parts, select, gate)


def local(tokens, router_weight, gate_weight, up_weight, down_weight, assignments, limits):
    local_rows = tokens.shape[0]
    experts = router_weight.shape[1]
    rings = lax.axis_size("y")
    shards = rings * CORES
    owners = lax.axis_size("exp")
    parts = lax.axis_size("tp")
    capacity = min(local_rows, max(2, 3 * local_rows * TOP // (2 * experts)))
    out_rows = local_rows // owners
    target = local_rows * shards * TOP / experts
    owner = lax.axis_index("exp")

    place = [jnp.reshape(lax.axis_index(axis), (1,)) for axis in ("exp", "tp")]
    select, main, share = route(*place, limits, assignments.T, tokens, capacity, SHARE, parts)
    rows = lax.all_gather(main, "y", axis=0, tiled=True)

    w_gate, w_up, w_down, tokens2, share, _ = lax.optimization_barrier(
        (gate_weight[0], up_weight[0], down_weight[0], tokens, share, main)
    )
    gate2, up2, down2 = swap_cores(w_gate), swap_cores(w_up), swap_cores(w_down)
    logits = lax.dot_general(
        router_weight, tokens2, (((0,), (1,)), ((), ())), preferred_element_type=jnp.float32
    )
    scores = SOFT_CAP * jnp.tanh(logits / SOFT_CAP)
    pieces = []
    for piece in range(3):
        pieces.append(lax.reduce_precision(scores, exponent_bits=8, mantissa_bits=7))
        scores = scores - pieces[-1]
    pieces = jnp.concatenate(pieces, axis=0).astype(jnp.bfloat16)
    count = pieces.shape[0]
    slots = TAIL * SHARE // local_rows
    pieces = jnp.pad(pieces, ((0, slots - count), (0, 0))).reshape(TAIL, SHARE)
    payload = jnp.concatenate([share, pieces], axis=0)
    near = lax.all_to_all(
        jnp.broadcast_to(payload, (rings,) + payload.shape), "y", 0, 0
    )
    own_share = near[:, :capacity].reshape(rings * capacity, SHARE)
    last = lax.all_gather(own_share, "tp", axis=0)

    tail = near[:, capacity:].reshape(rings, slots, local_rows)[:, :count]
    tail = jnp.sum(tail.reshape(rings, 3, experts, local_rows).astype(jnp.float32), axis=1)
    weights = jnp.exp(jnp.concatenate([tail, swap_cores(tail)], axis=0))
    weights = weights * (TOP / jnp.sum(weights, axis=1, keepdims=True))
    for repeat in range(ITERS):
        weights = weights * (target / jnp.sum(weights, axis=(0, 2), keepdims=True))
        weights = weights * (TOP / jnp.sum(weights, axis=1, keepdims=True))
    own = lax.dynamic_slice(weights, (lax.axis_index("y"), owner, 0), (1, 1, local_rows))[0]

    hidden = ffn(rows, last, w_gate, w_up, gate2, up2)
    full_hidden = lax.all_gather(hidden, "tp", axis=0)
    partial = down(full_hidden, w_down, down2)
    sums = lax.all_to_all(partial.reshape(rings, capacity, partial.shape[1]), "y", 0, 0)
    shares = weigh(sums, select, own)
    shares = lax.all_to_all(shares.reshape(owners, out_rows, shares.shape[1]), "exp", 0, 0)
    return jnp.sum(shares.astype(jnp.float32), axis=0).astype(jnp.bfloat16)


def solution(mesh):
    shape = mesh.devices.shape
    fine = Mesh(
        mesh.devices.reshape((shape[0] // CORES, CORES) + shape[1:]), ("y", "core", "exp", "tp")
    )
    tok = ("y", "core")
    placed = (
        P(tok, None),
        P(),
        P("exp", None, tok + ("tp",)),
        P("exp", None, tok + ("tp",)),
        P("exp", tok, "tp"),
        P(tok, None),
        P(tok, None),
    )
    return jax.shard_map(
        local, mesh=fine, in_specs=placed, out_specs=P(tok + ("exp",), "tp"), check_vma=False
    )
```

```python
import jax
import jax.numpy as jnp
from jax import lax
from jax.experimental import pallas as pl
from jax.experimental.pallas import tpu as pltpu
from jax.sharding import Mesh, PartitionSpec as P

TOP = 2
ITERS = 4
SOFT_CAP = 8.0
CORES = 2
ALL_VMEM = 64 << 20
FFN_VMEM = 60 << 20
SHARE = 256
TAIL = 16


def swap_cores(value):
    return lax.ppermute(value, "core", [(0, 1), (1, 0)])


def route_kernel(
    owner_ref, part_ref, limits_hbm, assign_hbm, tokens_hbm, select_ref, rows_hbm, share_ref,
    limits_ref, assign_ref, tokens_ref, own_ref, rows_ref, sems, out_sems
):
    width = tokens_ref.shape[1]
    share = own_ref.shape[1]
    chunks = out_sems.shape[0]
    parts = [pl.ds(index * (width // chunks), width // chunks) for index in range(chunks)]
    owner = owner_ref[0]
    first = pl.multiple_of(width + part_ref[0] * share, 128)
    small = [
        pltpu.make_async_copy(limits_hbm, limits_ref, sems.at[chunks]),
        pltpu.make_async_copy(assign_hbm, assign_ref, sems.at[chunks + 1]),
    ]
    copies = [
        pltpu.make_async_copy(tokens_hbm.at[:, part], tokens_ref.at[:, part], sems.at[index])
        for index, part in enumerate(parts)
    ]
    last = pltpu.make_async_copy(
        tokens_hbm.at[:, pl.ds(first, share)], own_ref, sems.at[chunks + 2]
    )
    for copy in small + copies + [last]:
        copy.start()
    capacity, count = select_ref.shape
    row = lax.broadcasted_iota(jnp.int32, (count, count), 0)
    column = lax.broadcasted_iota(jnp.int32, (count, count), 1)
    earlier = jnp.where(row < column, 1.0, 0.0).astype(jnp.bfloat16)
    slot_ids = lax.broadcasted_iota(jnp.int32, (capacity, count), 0)
    for copy in small:
        copy.wait()
    hit = jnp.sum(jnp.where(assign_ref[...] == owner, 1.0, 0.0), axis=0, keepdims=True)
    named = jnp.broadcast_to(hit, (16, count)).astype(jnp.bfloat16)
    slot = jnp.dot(named, earlier, preferred_element_type=jnp.float32)[:1].astype(jnp.int32)
    slot = jnp.where((hit > 0.0) & (slot < limits_ref[0, owner]), slot, -1)
    select = jnp.where(slot_ids == slot, 1.0, 0.0).astype(jnp.bfloat16)
    select_ref[...] = select
    outs = []
    for index, part in enumerate(parts):
        copies[index].wait()
        rows_ref[:, part] = jnp.dot(
            select, tokens_ref[:, part], preferred_element_type=jnp.float32
        ).astype(rows_ref.dtype)
        outs.append(
            pltpu.make_async_copy(
                rows_ref.at[:, part], rows_hbm.at[:, part], out_sems.at[index]
            )
        )
        outs[-1].start()
    last.wait()
    share_ref[...] = jnp.dot(
        select, own_ref[...], preferred_element_type=jnp.float32
    ).astype(share_ref.dtype)
    for copy in outs:
        copy.wait()


def route(owner, part, limits, assignments, tokens, capacity, share, parts, chunks=3):
    count = tokens.shape[0]
    width = tokens.shape[1] - parts * share
    far = pl.BlockSpec(memory_space=pltpu.HBM)
    near = pl.BlockSpec(memory_space=pltpu.VMEM)
    return pl.pallas_call(
        route_kernel,
        in_specs=[pl.BlockSpec(memory_space=pltpu.SMEM)] * 2 + [far] * 3,
        out_specs=[near, far, near],
        out_shape=[
            jax.ShapeDtypeStruct((capacity, count), jnp.bfloat16),
            jax.ShapeDtypeStruct((capacity, width), jnp.bfloat16),
            jax.ShapeDtypeStruct((capacity, share), jnp.bfloat16),
        ],
        scratch_shapes=[
            pltpu.SMEM(limits.shape, jnp.int32),
            pltpu.VMEM(assignments.shape, jnp.int32),
            pltpu.VMEM((count, width), jnp.bfloat16),
            pltpu.VMEM((count, share), jnp.bfloat16),
            pltpu.VMEM((capacity, width), jnp.bfloat16),
            pltpu.SemaphoreType.DMA((chunks + 3,)),
            pltpu.SemaphoreType.DMA((chunks,)),
        ],
        compiler_params=pltpu.CompilerParams(vmem_limit_bytes=ALL_VMEM),
        cost_estimate=pl.CostEstimate(
            flops=2 * capacity * count * (width + share),
            bytes_accessed=2 * (count + capacity) * (width + share),
            transcendentals=0,
        ),
        name="route",
    )(owner, part, limits, assignments, tokens)


def prepare_kernel(
    last_hbm, gate_hbm, up_hbm, gate2_hbm, up2_hbm, total_ref, last_ref, weight_ref, sems
):
    shares, _, share = last_ref.shape
    width, units = gate_hbm.shape
    tail = pl.ds(width - shares * share, shares * share)
    copies = [pltpu.make_async_copy(last_hbm, last_ref, sems.at[0])]
    for place, ref in enumerate((gate_hbm, up_hbm, gate2_hbm, up2_hbm)):
        copies.append(
            pltpu.make_async_copy(
                ref.at[tail, :], weight_ref.at[:, pl.ds(place * units, units)], sems.at[1 + place]
            )
        )
    for copy in copies:
        copy.start()
    for copy in copies:
        copy.wait()
    total = None
    for index in range(shares):
        product = jnp.dot(
            last_ref[index],
            weight_ref[pl.ds(index * share, share), :],
            preferred_element_type=jnp.float32,
        )
        total = product if index == 0 else total + product
    total_ref[...] = total


def prepare(last, gate, up, gate2, up2):
    shares, count, share = last.shape
    units = gate.shape[1]
    return pl.pallas_call(
        prepare_kernel,
        in_specs=[pl.BlockSpec(memory_space=pltpu.HBM)] * 5,
        out_specs=pl.BlockSpec(memory_space=pltpu.VMEM),
        out_shape=pltpu.VMEM((count, 4 * units), jnp.float32),
        scratch_shapes=[
            pltpu.VMEM(last.shape, jnp.bfloat16),
            pltpu.VMEM((shares * share, 4 * units), jnp.bfloat16),
            pltpu.SemaphoreType.DMA((5,)),
        ],
        compiler_params=pltpu.CompilerParams(vmem_limit_bytes=FFN_VMEM),
        cost_estimate=pl.CostEstimate(
            flops=8 * count * shares * share * units,
            bytes_accessed=2 * shares * share * (count + 4 * units) + 16 * count * units,
            transcendentals=0,
        ),
        name="prepare",
    )(last, gate, up, gate2, up2)


def ffn_kernel(
    rows_hbm, gate_hbm, up_hbm, gate2_hbm, up2_hbm, start_ref, out_ref, rows_ref, weight_ref, sems
):
    chunks, chunk, columns = weight_ref.shape
    units = columns // 4
    copies = []
    for index in range(chunks):
        part = pl.ds(index * chunk, chunk)
        ends = [(rows_hbm.at[:, part], rows_ref.at[index])]
        for place, ref in enumerate((gate_hbm, up_hbm, gate2_hbm, up2_hbm)):
            ends.append(
                (ref.at[part, :], weight_ref.at[index, :, pl.ds(place * units, units)])
            )
        copies.append(
            [
                pltpu.make_async_copy(source, sink, sems.at[index, place])
                for place, (source, sink) in enumerate(ends)
            ]
        )
    for group in copies:
        for copy in group:
            copy.start()
    total = start_ref[...]
    for index, group in enumerate(copies):
        for copy in group:
            copy.wait()
        total = total + jnp.dot(
            rows_ref[index], weight_ref[index], preferred_element_type=jnp.float32
        )
    for side in range(2):
        gate = total[:, 2 * side * units : (2 * side + 1) * units]
        up = total[:, (2 * side + 1) * units : (2 * side + 2) * units]
        hidden = gate / (1.0 + jnp.exp(-gate)) * up
        out_ref[:, side * units : (side + 1) * units] = hidden.astype(out_ref.dtype)


def ffn(rows, gate, up, gate2, up2, start, chunk=512):
    count, main = rows.shape
    units = gate.shape[1]
    near = pl.BlockSpec(memory_space=pltpu.VMEM)
    return pl.pallas_call(
        ffn_kernel,
        in_specs=[pl.BlockSpec(memory_space=pltpu.HBM)] * 5 + [near],
        out_specs=near,
        out_shape=pltpu.VMEM((count, 2 * units), jnp.bfloat16),
        scratch_shapes=[
            pltpu.VMEM((main // chunk, count, chunk), jnp.bfloat16),
            pltpu.VMEM((main // chunk, chunk, 4 * units), jnp.bfloat16),
            pltpu.SemaphoreType.DMA((main // chunk, 5)),
        ],
        compiler_params=pltpu.CompilerParams(vmem_limit_bytes=FFN_VMEM),
        cost_estimate=pl.CostEstimate(
            flops=8 * count * main * units,
            bytes_accessed=2 * count * main + 8 * main * units,
            transcendentals=2 * count * units,
        ),
        name="ffn",
    )(rows, gate, up, gate2, up2, start)


def down_kernel(hidden_ref, down_ref, down2_ref, out_ref):
    parts = hidden_ref.shape[0]
    units = down_ref.shape[0] // parts
    total = None
    for index in range(parts):
        part = pl.ds(index * units, units)
        both = jnp.concatenate([down_ref[part, :], down2_ref[part, :]], axis=0)
        product = jnp.dot(hidden_ref[index], both, preferred_element_type=jnp.float32)
        total = product if index == 0 else total + product
    out_ref[...] = total.astype(out_ref.dtype)


def down(hidden, weight, weight2):
    parts, count, units = hidden.shape
    columns = weight.shape[1]
    return pl.pallas_call(
        down_kernel,
        out_shape=pltpu.VMEM((count, columns), jnp.bfloat16),
        compiler_params=pltpu.CompilerParams(vmem_limit_bytes=24 << 20),
        cost_estimate=pl.CostEstimate(
            flops=2 * parts * count * units * columns,
            bytes_accessed=2 * parts * units * (count + columns) + 2 * count * columns,
            transcendentals=0,
        ),
        name="down",
    )(hidden, weight, weight2)


def weigh_kernel(parts_ref, select_ref, gate_ref, out_ref):
    select = select_ref[...]
    total = jnp.sum(parts_ref[...].astype(jnp.float32), axis=0).astype(jnp.bfloat16)
    gate = jnp.sum(select.astype(jnp.float32) * gate_ref[...], axis=1, keepdims=True)
    weighted = (total.astype(jnp.float32) * gate).astype(jnp.bfloat16)
    out_ref[...] = lax.dot_general(
        select, weighted, (((0,), (0,)), ((), ())), preferred_element_type=jnp.float32
    ).astype(out_ref.dtype)


def weigh(parts, select, gate):
    count = select.shape[1]
    columns = parts.shape[2]
    return pl.pallas_call(
        weigh_kernel,
        out_shape=jax.ShapeDtypeStruct((count, columns), jnp.bfloat16),
        compiler_params=pltpu.CompilerParams(vmem_limit_bytes=24 << 20),
        cost_estimate=pl.CostEstimate(
            flops=2 * count * select.shape[0] * columns,
            bytes_accessed=2 * parts.size + 2 * count * columns,
            transcendentals=0,
        ),
        name="weigh",
    )(parts, select, gate)


def local(tokens, router_weight, gate_weight, up_weight, down_weight, assignments, limits):
    local_rows = tokens.shape[0]
    experts = router_weight.shape[1]
    rings = lax.axis_size("y")
    shards = rings * CORES
    owners = lax.axis_size("exp")
    parts = lax.axis_size("tp")
    capacity = min(local_rows, max(2, 3 * local_rows * TOP // (2 * experts)))
    out_rows = local_rows // owners
    target = local_rows * shards * TOP / experts
    owner = lax.axis_index("exp")

    place = [jnp.reshape(lax.axis_index(axis), (1,)) for axis in ("exp", "tp")]
    select, main, share = route(*place, limits, assignments.T, tokens, capacity, SHARE, parts)
    rows = lax.all_gather(main, "y", axis=0, tiled=True)

    w_gate, w_up, w_down, tokens2, share, _ = lax.optimization_barrier(
        (gate_weight[0], up_weight[0], down_weight[0], tokens, share, main)
    )
    gate2, up2, down2 = swap_cores(w_gate), swap_cores(w_up), swap_cores(w_down)
    logits = lax.dot_general(
        router_weight, tokens2, (((0,), (1,)), ((), ())), preferred_element_type=jnp.float32
    )
    scores = SOFT_CAP * jnp.tanh(logits / SOFT_CAP)
    pieces = []
    for piece in range(3):
        pieces.append(lax.reduce_precision(scores, exponent_bits=8, mantissa_bits=7))
        scores = scores - pieces[-1]
    pieces = jnp.concatenate(pieces, axis=0).astype(jnp.bfloat16)
    count = pieces.shape[0]
    slots = TAIL * SHARE // local_rows
    pieces = jnp.pad(pieces, ((0, slots - count), (0, 0))).reshape(TAIL, SHARE)
    payload = jnp.concatenate([share, pieces], axis=0)
    near = lax.all_to_all(
        jnp.broadcast_to(payload, (rings,) + payload.shape), "y", 0, 0
    )
    own_share = near[:, :capacity].reshape(rings * capacity, SHARE)
    last = lax.all_gather(own_share, "tp", axis=0)

    tail = near[:, capacity:].reshape(rings, slots, local_rows)[:, :count]
    tail = jnp.sum(tail.reshape(rings, 3, experts, local_rows).astype(jnp.float32), axis=1)
    weights = jnp.exp(jnp.concatenate([tail, swap_cores(tail)], axis=0))
    weights = weights * (TOP / jnp.sum(weights, axis=1, keepdims=True))
    for repeat in range(ITERS):
        weights = weights * (target / jnp.sum(weights, axis=(0, 2), keepdims=True))
        weights = weights * (TOP / jnp.sum(weights, axis=1, keepdims=True))
    own = lax.dynamic_slice(weights, (lax.axis_index("y"), owner, 0), (1, 1, local_rows))[0]

    start = prepare(last, w_gate, w_up, gate2, up2)
    start = pltpu.with_memory_space_constraint(start, pltpu.VMEM)
    hidden = ffn(rows, w_gate, w_up, gate2, up2, start)
    full_hidden = lax.all_gather(hidden, "tp", axis=0)
    partial = down(full_hidden, w_down, down2)
    sums = lax.all_to_all(partial.reshape(rings, capacity, partial.shape[1]), "y", 0, 0)
    shares = weigh(sums, select, own)
    shares = lax.all_to_all(shares.reshape(owners, out_rows, shares.shape[1]), "exp", 0, 0)
    return jnp.sum(shares.astype(jnp.float32), axis=0).astype(jnp.bfloat16)


def solution(mesh):
    shape = mesh.devices.shape
    fine = Mesh(
        mesh.devices.reshape((shape[0] // CORES, CORES) + shape[1:]), ("y", "core", "exp", "tp")
    )
    tok = ("y", "core")
    placed = (
        P(tok, None),
        P(),
        P("exp", None, tok + ("tp",)),
        P("exp", None, tok + ("tp",)),
        P("exp", tok, "tp"),
        P(tok, None),
        P(tok, None),
    )
    return jax.shard_map(
        local, mesh=fine, in_specs=placed, out_specs=P(tok + ("exp",), "tp"), check_vma=False
    )
```

```python
import jax
import jax.numpy as jnp
from jax import lax
from jax.experimental import pallas as pl
from jax.experimental.pallas import tpu as pltpu
from jax.sharding import Mesh, PartitionSpec as P

TOP = 2
ITERS = 4
SOFT_CAP = 8.0
CORES = 2
ALL_VMEM = 64 << 20
FFN_VMEM = 60 << 20
SHARE = 256
TAIL = 16


def swap_cores(value):
    return lax.ppermute(value, "core", [(0, 1), (1, 0)])


def route_kernel(
    owner_ref, part_ref, limits_hbm, assign_hbm, tokens_hbm, select_ref, rows_hbm, share_ref,
    limits_ref, assign_ref, tokens_ref, own_ref, rows_ref, sems, out_sems
):
    width = tokens_ref.shape[1]
    share = own_ref.shape[1]
    chunks = out_sems.shape[0]
    parts = [pl.ds(index * (width // chunks), width // chunks) for index in range(chunks)]
    owner = owner_ref[0]
    first = pl.multiple_of(width + part_ref[0] * share, 128)
    small = [
        pltpu.make_async_copy(limits_hbm, limits_ref, sems.at[chunks]),
        pltpu.make_async_copy(assign_hbm, assign_ref, sems.at[chunks + 1]),
    ]
    copies = [
        pltpu.make_async_copy(tokens_hbm.at[:, part], tokens_ref.at[:, part], sems.at[index])
        for index, part in enumerate(parts)
    ]
    last = pltpu.make_async_copy(
        tokens_hbm.at[:, pl.ds(first, share)], own_ref, sems.at[chunks + 2]
    )
    for copy in small + copies + [last]:
        copy.start()
    capacity, count = select_ref.shape
    row = lax.broadcasted_iota(jnp.int32, (count, count), 0)
    column = lax.broadcasted_iota(jnp.int32, (count, count), 1)
    earlier = jnp.where(row < column, 1.0, 0.0).astype(jnp.bfloat16)
    slot_ids = lax.broadcasted_iota(jnp.int32, (capacity, count), 0)
    for copy in small:
        copy.wait()
    hit = jnp.sum(jnp.where(assign_ref[...] == owner, 1.0, 0.0), axis=0, keepdims=True)
    named = jnp.broadcast_to(hit, (16, count)).astype(jnp.bfloat16)
    slot = jnp.dot(named, earlier, preferred_element_type=jnp.float32)[:1].astype(jnp.int32)
    slot = jnp.where((hit > 0.0) & (slot < limits_ref[0, owner]), slot, -1)
    select = jnp.where(slot_ids == slot, 1.0, 0.0).astype(jnp.bfloat16)
    select_ref[...] = select
    outs = []
    for index, part in enumerate(parts):
        copies[index].wait()
        rows_ref[:, part] = jnp.dot(
            select, tokens_ref[:, part], preferred_element_type=jnp.float32
        ).astype(rows_ref.dtype)
        outs.append(
            pltpu.make_async_copy(
                rows_ref.at[:, part], rows_hbm.at[:, part], out_sems.at[index]
            )
        )
        outs[-1].start()
    last.wait()
    share_ref[...] = jnp.dot(
        select, own_ref[...], preferred_element_type=jnp.float32
    ).astype(share_ref.dtype)
    for copy in outs:
        copy.wait()


def route(owner, part, limits, assignments, tokens, capacity, share, parts, chunks=3):
    count = tokens.shape[0]
    width = tokens.shape[1] - parts * share
    far = pl.BlockSpec(memory_space=pltpu.HBM)
    near = pl.BlockSpec(memory_space=pltpu.VMEM)
    return pl.pallas_call(
        route_kernel,
        in_specs=[pl.BlockSpec(memory_space=pltpu.SMEM)] * 2 + [far] * 3,
        out_specs=[near, far, near],
        out_shape=[
            jax.ShapeDtypeStruct((capacity, count), jnp.bfloat16),
            jax.ShapeDtypeStruct((capacity, width), jnp.bfloat16),
            jax.ShapeDtypeStruct((capacity, share), jnp.bfloat16),
        ],
        scratch_shapes=[
            pltpu.SMEM(limits.shape, jnp.int32),
            pltpu.VMEM(assignments.shape, jnp.int32),
            pltpu.VMEM((count, width), jnp.bfloat16),
            pltpu.VMEM((count, share), jnp.bfloat16),
            pltpu.VMEM((capacity, width), jnp.bfloat16),
            pltpu.SemaphoreType.DMA((chunks + 3,)),
            pltpu.SemaphoreType.DMA((chunks,)),
        ],
        compiler_params=pltpu.CompilerParams(vmem_limit_bytes=ALL_VMEM),
        cost_estimate=pl.CostEstimate(
            flops=2 * capacity * count * (width + share),
            bytes_accessed=2 * (count + capacity) * (width + share),
            transcendentals=0,
        ),
        name="route",
    )(owner, part, limits, assignments, tokens)


def prepare_kernel(
    last_hbm, gate_hbm, up_hbm, gate2_hbm, up2_hbm, total_ref, last_ref, weight_ref, sems
):
    shares, _, share = last_ref.shape
    width, units = gate_hbm.shape
    tail = pl.ds(width - shares * share, shares * share)
    copies = [pltpu.make_async_copy(last_hbm, last_ref, sems.at[0])]
    for place, ref in enumerate((gate_hbm, up_hbm, gate2_hbm, up2_hbm)):
        copies.append(
            pltpu.make_async_copy(
                ref.at[tail, :], weight_ref.at[:, pl.ds(place * units, units)], sems.at[1 + place]
            )
        )
    for copy in copies:
        copy.start()
    for copy in copies:
        copy.wait()
    total = None
    for index in range(shares):
        product = jnp.dot(
            last_ref[index],
            weight_ref[pl.ds(index * share, share), :],
            preferred_element_type=jnp.float32,
        )
        total = product if index == 0 else total + product
    total_ref[...] = total


def prepare(last, gate, up, gate2, up2):
    shares, count, share = last.shape
    units = gate.shape[1]
    return pl.pallas_call(
        prepare_kernel,
        in_specs=[pl.BlockSpec(memory_space=pltpu.HBM)] * 5,
        out_specs=pl.BlockSpec(memory_space=pltpu.VMEM),
        out_shape=pltpu.VMEM((count, 4 * units), jnp.float32),
        scratch_shapes=[
            pltpu.VMEM(last.shape, jnp.bfloat16),
            pltpu.VMEM((shares * share, 4 * units), jnp.bfloat16),
            pltpu.SemaphoreType.DMA((5,)),
        ],
        compiler_params=pltpu.CompilerParams(vmem_limit_bytes=FFN_VMEM),
        cost_estimate=pl.CostEstimate(
            flops=8 * count * shares * share * units,
            bytes_accessed=2 * shares * share * (count + 4 * units) + 16 * count * units,
            transcendentals=0,
        ),
        name="prepare",
    )(last, gate, up, gate2, up2)


def ffn_kernel(
    rows_hbm, gate_hbm, up_hbm, gate2_hbm, up2_hbm, start_ref, out_ref, rows_ref, weight_ref, sems
):
    chunks, chunk, columns = weight_ref.shape
    units = columns // 4
    copies = []
    for index in range(chunks):
        part = pl.ds(index * chunk, chunk)
        ends = [(rows_hbm.at[:, part], rows_ref.at[index])]
        for place, ref in enumerate((gate_hbm, up_hbm, gate2_hbm, up2_hbm)):
            ends.append(
                (ref.at[part, :], weight_ref.at[index, :, pl.ds(place * units, units)])
            )
        copies.append(
            [
                pltpu.make_async_copy(source, sink, sems.at[index, place])
                for place, (source, sink) in enumerate(ends)
            ]
        )
    for group in copies:
        for copy in group:
            copy.start()
    total = start_ref[...]
    for index, group in enumerate(copies):
        for copy in group:
            copy.wait()
        total = total + jnp.dot(
            rows_ref[index], weight_ref[index], preferred_element_type=jnp.float32
        )
    for side in range(2):
        gate = total[:, 2 * side * units : (2 * side + 1) * units]
        up = total[:, (2 * side + 1) * units : (2 * side + 2) * units]
        hidden = gate / (1.0 + jnp.exp(-gate)) * up
        out_ref[:, side * units : (side + 1) * units] = hidden.astype(out_ref.dtype)


def ffn(rows, gate, up, gate2, up2, start, chunk=512):
    count, main = rows.shape
    units = gate.shape[1]
    near = pl.BlockSpec(memory_space=pltpu.VMEM)
    return pl.pallas_call(
        ffn_kernel,
        in_specs=[pl.BlockSpec(memory_space=pltpu.HBM)] * 5 + [near],
        out_specs=near,
        out_shape=pltpu.VMEM((count, 2 * units), jnp.bfloat16),
        scratch_shapes=[
            pltpu.VMEM((main // chunk, count, chunk), jnp.bfloat16),
            pltpu.VMEM((main // chunk, chunk, 4 * units), jnp.bfloat16),
            pltpu.SemaphoreType.DMA((main // chunk, 5)),
        ],
        compiler_params=pltpu.CompilerParams(vmem_limit_bytes=FFN_VMEM),
        cost_estimate=pl.CostEstimate(
            flops=8 * count * main * units,
            bytes_accessed=2 * count * main + 8 * main * units,
            transcendentals=2 * count * units,
        ),
        name="ffn",
    )(rows, gate, up, gate2, up2, start)


def down_kernel(hidden_ref, down_ref, down2_ref, out_ref):
    parts = hidden_ref.shape[0]
    units = down_ref.shape[0] // parts
    total = None
    for index in range(parts):
        part = pl.ds(index * units, units)
        both = jnp.concatenate([down_ref[part, :], down2_ref[part, :]], axis=0)
        product = jnp.dot(hidden_ref[index], both, preferred_element_type=jnp.float32)
        total = product if index == 0 else total + product
    out_ref[...] = total.astype(out_ref.dtype)


def down(hidden, weight, weight2):
    parts, count, units = hidden.shape
    columns = weight.shape[1]
    return pl.pallas_call(
        down_kernel,
        out_shape=pltpu.VMEM((count, columns), jnp.bfloat16),
        compiler_params=pltpu.CompilerParams(vmem_limit_bytes=24 << 20),
        cost_estimate=pl.CostEstimate(
            flops=2 * parts * count * units * columns,
            bytes_accessed=2 * parts * units * (count + columns) + 2 * count * columns,
            transcendentals=0,
        ),
        name="down",
    )(hidden, weight, weight2)


def weigh_kernel(parts_ref, select_ref, gate_ref, out_ref):
    select = select_ref[...]
    total = jnp.sum(parts_ref[...].astype(jnp.float32), axis=0).astype(jnp.bfloat16)
    gate = jnp.sum(select.astype(jnp.float32) * gate_ref[...], axis=1, keepdims=True)
    weighted = (total.astype(jnp.float32) * gate).astype(jnp.bfloat16)
    out_ref[...] = lax.dot_general(
        select, weighted, (((0,), (0,)), ((), ())), preferred_element_type=jnp.float32
    ).astype(out_ref.dtype)


def weigh(parts, select, gate):
    count = select.shape[1]
    columns = parts.shape[2]
    return pl.pallas_call(
        weigh_kernel,
        out_shape=jax.ShapeDtypeStruct((count, columns), jnp.bfloat16),
        compiler_params=pltpu.CompilerParams(vmem_limit_bytes=24 << 20),
        cost_estimate=pl.CostEstimate(
            flops=2 * count * select.shape[0] * columns,
            bytes_accessed=2 * parts.size + 2 * count * columns,
            transcendentals=0,
        ),
        name="weigh",
    )(parts, select, gate)


def local(tokens, router_weight, gate_weight, up_weight, down_weight, assignments, limits):
    local_rows = tokens.shape[0]
    experts = router_weight.shape[1]
    rings = lax.axis_size("y")
    shards = rings * CORES
    owners = lax.axis_size("exp")
    parts = lax.axis_size("tp")
    capacity = min(local_rows, max(2, 3 * local_rows * TOP // (2 * experts)))
    out_rows = local_rows // owners
    target = local_rows * shards * TOP / experts
    owner = lax.axis_index("exp")

    place = [jnp.reshape(lax.axis_index(axis), (1,)) for axis in ("exp", "tp")]
    select, main, share = route(*place, limits, assignments.T, tokens, capacity, SHARE, parts)
    rows = lax.all_gather(main, "y", axis=0, tiled=True)

    w_gate, w_up, w_down, tokens2, share, _ = lax.optimization_barrier(
        (gate_weight[0], up_weight[0], down_weight[0], tokens, share, main)
    )
    gate2, up2, down2 = swap_cores(w_gate), swap_cores(w_up), swap_cores(w_down)
    logits = lax.dot_general(
        router_weight, tokens2, (((0,), (1,)), ((), ())), preferred_element_type=jnp.float32
    )
    scores = SOFT_CAP * jnp.tanh(logits / SOFT_CAP)
    pieces = []
    for piece in range(3):
        pieces.append(lax.reduce_precision(scores, exponent_bits=8, mantissa_bits=7))
        scores = scores - pieces[-1]
    pieces = jnp.concatenate(pieces, axis=0).astype(jnp.bfloat16)
    count = pieces.shape[0]
    slots = TAIL * SHARE // local_rows
    pieces = jnp.pad(pieces, ((0, slots - count), (0, 0))).reshape(TAIL, SHARE)
    payload = jnp.concatenate([share, pieces], axis=0)
    near = lax.all_to_all(
        jnp.broadcast_to(payload, (rings,) + payload.shape), "y", 0, 0
    )
    own_share = near[:, :capacity].reshape(rings * capacity, SHARE)
    last = lax.all_gather(own_share, "tp", axis=0)

    tail = near[:, capacity:].reshape(rings, slots, local_rows)[:, :count]
    tail = jnp.sum(tail.reshape(rings, 3, experts, local_rows).astype(jnp.float32), axis=1)
    weights = jnp.exp(jnp.concatenate([tail, swap_cores(tail)], axis=0))
    weights = weights * (TOP / jnp.sum(weights, axis=1, keepdims=True))
    for repeat in range(ITERS):
        weights = weights * (target / jnp.sum(weights, axis=(0, 2), keepdims=True))
        weights = weights * (TOP / jnp.sum(weights, axis=1, keepdims=True))
    own = lax.dynamic_slice(weights, (lax.axis_index("y"), owner, 0), (1, 1, local_rows))[0]

    start = prepare(last, w_gate, w_up, gate2, up2)
    start = pltpu.with_memory_space_constraint(start, pltpu.VMEM)
    own, start = lax.optimization_barrier((own, start))
    hidden = ffn(rows, w_gate, w_up, gate2, up2, start)
    full_hidden = lax.all_gather(hidden, "tp", axis=0)
    partial = down(full_hidden, w_down, down2)
    sums = lax.all_to_all(partial.reshape(rings, capacity, partial.shape[1]), "y", 0, 0)
    shares = weigh(sums, select, own)
    shares = lax.all_to_all(shares.reshape(owners, out_rows, shares.shape[1]), "exp", 0, 0)
    return jnp.sum(shares.astype(jnp.float32), axis=0).astype(jnp.bfloat16)


def solution(mesh):
    shape = mesh.devices.shape
    fine = Mesh(
        mesh.devices.reshape((shape[0] // CORES, CORES) + shape[1:]), ("y", "core", "exp", "tp")
    )
    tok = ("y", "core")
    placed = (
        P(tok, None),
        P(),
        P("exp", None, tok + ("tp",)),
        P("exp", None, tok + ("tp",)),
        P("exp", tok, "tp"),
        P(tok, None),
        P(tok, None),
    )
    return jax.shard_map(
        local, mesh=fine, in_specs=placed, out_specs=P(tok + ("exp",), "tp"), check_vma=False
    )
```

```python
import jax
import jax.numpy as jnp
from jax import lax
from jax.experimental import pallas as pl
from jax.experimental.pallas import tpu as pltpu
from jax.sharding import Mesh, PartitionSpec as P

TOP = 2
ITERS = 4
SOFT_CAP = 8.0
CORES = 2
ALL_VMEM = 64 << 20
FFN_VMEM = 60 << 20
SHARE = 256
TAIL = 16


def swap_cores(value):
    return lax.ppermute(value, "core", [(0, 1), (1, 0)])


def route_kernel(
    owner_ref, part_ref, limits_hbm, assign_hbm, tokens_hbm, select_ref, rows_hbm, share_ref,
    limits_ref, assign_ref, tokens_ref, own_ref, rows_ref, sems, out_sems
):
    width = tokens_ref.shape[1]
    share = own_ref.shape[1]
    chunks = out_sems.shape[0]
    parts = [pl.ds(index * (width // chunks), width // chunks) for index in range(chunks)]
    owner = owner_ref[0]
    first = pl.multiple_of(width + part_ref[0] * share, 128)
    small = [
        pltpu.make_async_copy(limits_hbm, limits_ref, sems.at[chunks]),
        pltpu.make_async_copy(assign_hbm, assign_ref, sems.at[chunks + 1]),
    ]
    copies = [
        pltpu.make_async_copy(tokens_hbm.at[:, part], tokens_ref.at[:, part], sems.at[index])
        for index, part in enumerate(parts)
    ]
    last = pltpu.make_async_copy(
        tokens_hbm.at[:, pl.ds(first, share)], own_ref, sems.at[chunks + 2]
    )
    for copy in small + copies + [last]:
        copy.start()
    capacity, count = select_ref.shape
    row = lax.broadcasted_iota(jnp.int32, (count, count), 0)
    column = lax.broadcasted_iota(jnp.int32, (count, count), 1)
    earlier = jnp.where(row < column, 1.0, 0.0).astype(jnp.bfloat16)
    slot_ids = lax.broadcasted_iota(jnp.int32, (capacity, count), 0)
    for copy in small:
        copy.wait()
    hit = jnp.sum(jnp.where(assign_ref[...] == owner, 1.0, 0.0), axis=0, keepdims=True)
    named = jnp.broadcast_to(hit, (16, count)).astype(jnp.bfloat16)
    slot = jnp.dot(named, earlier, preferred_element_type=jnp.float32)[:1].astype(jnp.int32)
    slot = jnp.where((hit > 0.0) & (slot < limits_ref[0, owner]), slot, -1)
    select = jnp.where(slot_ids == slot, 1.0, 0.0).astype(jnp.bfloat16)
    select_ref[...] = select
    outs = []
    for index, part in enumerate(parts):
        copies[index].wait()
        rows_ref[:, part] = jnp.dot(
            select, tokens_ref[:, part], preferred_element_type=jnp.float32
        ).astype(rows_ref.dtype)
        outs.append(
            pltpu.make_async_copy(
                rows_ref.at[:, part], rows_hbm.at[:, part], out_sems.at[index]
            )
        )
        outs[-1].start()
    last.wait()
    share_ref[...] = jnp.dot(
        select, own_ref[...], preferred_element_type=jnp.float32
    ).astype(share_ref.dtype)
    for copy in outs:
        copy.wait()


def route(owner, part, limits, assignments, tokens, capacity, share, parts, chunks=3):
    count = tokens.shape[0]
    width = tokens.shape[1] - parts * share
    far = pl.BlockSpec(memory_space=pltpu.HBM)
    near = pl.BlockSpec(memory_space=pltpu.VMEM)
    return pl.pallas_call(
        route_kernel,
        in_specs=[pl.BlockSpec(memory_space=pltpu.SMEM)] * 2 + [far] * 3,
        out_specs=[near, far, near],
        out_shape=[
            jax.ShapeDtypeStruct((capacity, count), jnp.bfloat16),
            jax.ShapeDtypeStruct((capacity, width), jnp.bfloat16),
            jax.ShapeDtypeStruct((capacity, share), jnp.bfloat16),
        ],
        scratch_shapes=[
            pltpu.SMEM(limits.shape, jnp.int32),
            pltpu.VMEM(assignments.shape, jnp.int32),
            pltpu.VMEM((count, width), jnp.bfloat16),
            pltpu.VMEM((count, share), jnp.bfloat16),
            pltpu.VMEM((capacity, width), jnp.bfloat16),
            pltpu.SemaphoreType.DMA((chunks + 3,)),
            pltpu.SemaphoreType.DMA((chunks,)),
        ],
        compiler_params=pltpu.CompilerParams(vmem_limit_bytes=ALL_VMEM),
        cost_estimate=pl.CostEstimate(
            flops=2 * capacity * count * (width + share),
            bytes_accessed=2 * (count + capacity) * (width + share),
            transcendentals=0,
        ),
        name="route",
    )(owner, part, limits, assignments, tokens)


def prepare_kernel(
    last_hbm, gate_hbm, up_hbm, gate2_hbm, up2_hbm, total_ref, last_ref, weight_ref, sems
):
    shares, _, share = last_ref.shape
    width, units = gate_hbm.shape
    tail = pl.ds(width - shares * share, shares * share)
    copies = [pltpu.make_async_copy(last_hbm, last_ref, sems.at[0])]
    for place, ref in enumerate((gate_hbm, up_hbm, gate2_hbm, up2_hbm)):
        copies.append(
            pltpu.make_async_copy(
                ref.at[tail, :], weight_ref.at[:, pl.ds(place * units, units)], sems.at[1 + place]
            )
        )
    for copy in copies:
        copy.start()
    for copy in copies:
        copy.wait()
    total = None
    for index in range(shares):
        product = jnp.dot(
            last_ref[index],
            weight_ref[pl.ds(index * share, share), :],
            preferred_element_type=jnp.float32,
        )
        total = product if index == 0 else total + product
    total_ref[...] = total


def prepare(last, gate, up, gate2, up2):
    shares, count, share = last.shape
    units = gate.shape[1]
    return pl.pallas_call(
        prepare_kernel,
        in_specs=[pl.BlockSpec(memory_space=pltpu.HBM)] * 5,
        out_specs=pl.BlockSpec(memory_space=pltpu.VMEM),
        out_shape=pltpu.VMEM((count, 4 * units), jnp.float32),
        scratch_shapes=[
            pltpu.VMEM(last.shape, jnp.bfloat16),
            pltpu.VMEM((shares * share, 4 * units), jnp.bfloat16),
            pltpu.SemaphoreType.DMA((5,)),
        ],
        compiler_params=pltpu.CompilerParams(vmem_limit_bytes=FFN_VMEM),
        cost_estimate=pl.CostEstimate(flops=1, bytes_accessed=1, transcendentals=0),
        name="prepare",
    )(last, gate, up, gate2, up2)


def ffn_kernel(
    rows_hbm, gate_hbm, up_hbm, gate2_hbm, up2_hbm, start_ref, out_ref, rows_ref, weight_ref, sems
):
    chunks, chunk, columns = weight_ref.shape
    units = columns // 4
    copies = []
    for index in range(chunks):
        part = pl.ds(index * chunk, chunk)
        ends = [(rows_hbm.at[:, part], rows_ref.at[index])]
        for place, ref in enumerate((gate_hbm, up_hbm, gate2_hbm, up2_hbm)):
            ends.append(
                (ref.at[part, :], weight_ref.at[index, :, pl.ds(place * units, units)])
            )
        copies.append(
            [
                pltpu.make_async_copy(source, sink, sems.at[index, place])
                for place, (source, sink) in enumerate(ends)
            ]
        )
    for group in copies:
        for copy in group:
            copy.start()
    total = start_ref[...]
    for index, group in enumerate(copies):
        for copy in group:
            copy.wait()
        total = total + jnp.dot(
            rows_ref[index], weight_ref[index], preferred_element_type=jnp.float32
        )
    for side in range(2):
        gate = total[:, 2 * side * units : (2 * side + 1) * units]
        up = total[:, (2 * side + 1) * units : (2 * side + 2) * units]
        hidden = gate / (1.0 + jnp.exp(-gate)) * up
        out_ref[:, side * units : (side + 1) * units] = hidden.astype(out_ref.dtype)


def ffn(rows, gate, up, gate2, up2, start, chunk=512):
    count, main = rows.shape
    units = gate.shape[1]
    near = pl.BlockSpec(memory_space=pltpu.VMEM)
    return pl.pallas_call(
        ffn_kernel,
        in_specs=[pl.BlockSpec(memory_space=pltpu.HBM)] * 5 + [near],
        out_specs=near,
        out_shape=pltpu.VMEM((count, 2 * units), jnp.bfloat16),
        scratch_shapes=[
            pltpu.VMEM((main // chunk, count, chunk), jnp.bfloat16),
            pltpu.VMEM((main // chunk, chunk, 4 * units), jnp.bfloat16),
            pltpu.SemaphoreType.DMA((main // chunk, 5)),
        ],
        compiler_params=pltpu.CompilerParams(vmem_limit_bytes=FFN_VMEM),
        cost_estimate=pl.CostEstimate(
            flops=8 * count * main * units,
            bytes_accessed=2 * count * main + 8 * main * units,
            transcendentals=2 * count * units,
        ),
        name="ffn",
    )(rows, gate, up, gate2, up2, start)


def down_kernel(hidden_ref, down_ref, down2_ref, out_ref):
    parts = hidden_ref.shape[0]
    units = down_ref.shape[0] // parts
    total = None
    for index in range(parts):
        part = pl.ds(index * units, units)
        both = jnp.concatenate([down_ref[part, :], down2_ref[part, :]], axis=0)
        product = jnp.dot(hidden_ref[index], both, preferred_element_type=jnp.float32)
        total = product if index == 0 else total + product
    out_ref[...] = total.astype(out_ref.dtype)


def down(hidden, weight, weight2):
    parts, count, units = hidden.shape
    columns = weight.shape[1]
    return pl.pallas_call(
        down_kernel,
        out_shape=pltpu.VMEM((count, columns), jnp.bfloat16),
        compiler_params=pltpu.CompilerParams(vmem_limit_bytes=24 << 20),
        cost_estimate=pl.CostEstimate(
            flops=2 * parts * count * units * columns,
            bytes_accessed=2 * parts * units * (count + columns) + 2 * count * columns,
            transcendentals=0,
        ),
        name="down",
    )(hidden, weight, weight2)


def balance_kernel(place_ref, mine_ref, other_ref, gate_ref, kept_ref):
    shards, experts, count = mine_ref.shape
    target = 2.0 * shards * count * TOP / experts
    weights = jnp.exp(jnp.concatenate([mine_ref[...], other_ref[...]], axis=0))
    weights = weights * (TOP / jnp.sum(weights, axis=1, keepdims=True))
    for repeat in range(ITERS):
        column = jnp.sum(jnp.sum(weights, axis=0, keepdims=True), axis=2, keepdims=True)
        weights = weights * (target / column)
        weights = weights * (TOP / jnp.sum(weights, axis=1, keepdims=True))
    kept_ref[...] = weights[:shards]
    gate_ref[...] = kept_ref[place_ref[0], pl.ds(place_ref[1], 1), :]


def balance(place, mine, other):
    near = pl.BlockSpec(memory_space=pltpu.VMEM)
    return pl.pallas_call(
        balance_kernel,
        in_specs=[pl.BlockSpec(memory_space=pltpu.SMEM), near, near],
        out_specs=near,
        out_shape=jax.ShapeDtypeStruct((1, mine.shape[2]), jnp.float32),
        scratch_shapes=[pltpu.VMEM(mine.shape, jnp.float32)],
        compiler_params=pltpu.CompilerParams(vmem_limit_bytes=24 << 20),
        cost_estimate=pl.CostEstimate(flops=1, bytes_accessed=1, transcendentals=0),
        name="balance",
    )(place, mine, other)


def weigh_kernel(parts_ref, select_ref, gate_ref, out_ref):
    select = select_ref[...]
    total = jnp.sum(parts_ref[...].astype(jnp.float32), axis=0).astype(jnp.bfloat16)
    gate = jnp.sum(select.astype(jnp.float32) * gate_ref[...], axis=1, keepdims=True)
    weighted = (total.astype(jnp.float32) * gate).astype(jnp.bfloat16)
    out_ref[...] = lax.dot_general(
        select, weighted, (((0,), (0,)), ((), ())), preferred_element_type=jnp.float32
    ).astype(out_ref.dtype)


def weigh(parts, select, gate):
    count = select.shape[1]
    columns = parts.shape[2]
    return pl.pallas_call(
        weigh_kernel,
        out_shape=jax.ShapeDtypeStruct((count, columns), jnp.bfloat16),
        compiler_params=pltpu.CompilerParams(vmem_limit_bytes=24 << 20),
        cost_estimate=pl.CostEstimate(
            flops=2 * count * select.shape[0] * columns,
            bytes_accessed=2 * parts.size + 2 * count * columns,
            transcendentals=0,
        ),
        name="weigh",
    )(parts, select, gate)


def local(tokens, router_weight, gate_weight, up_weight, down_weight, assignments, limits):
    local_rows = tokens.shape[0]
    experts = router_weight.shape[1]
    rings = lax.axis_size("y")
    owners = lax.axis_size("exp")
    parts = lax.axis_size("tp")
    capacity = min(local_rows, max(2, 3 * local_rows * TOP // (2 * experts)))
    out_rows = local_rows // owners
    owner = lax.axis_index("exp")

    place = [jnp.reshape(lax.axis_index(axis), (1,)) for axis in ("exp", "tp")]
    select, main, share = route(*place, limits, assignments.T, tokens, capacity, SHARE, parts)
    rows = lax.all_gather(main, "y", axis=0, tiled=True)

    w_gate, w_up, w_down, tokens2, share, _ = lax.optimization_barrier(
        (gate_weight[0], up_weight[0], down_weight[0], tokens, share, main)
    )
    gate2, up2, down2 = swap_cores(w_gate), swap_cores(w_up), swap_cores(w_down)
    logits = lax.dot_general(
        router_weight, tokens2, (((0,), (1,)), ((), ())), preferred_element_type=jnp.float32
    )
    scores = SOFT_CAP * jnp.tanh(logits / SOFT_CAP)
    pieces = []
    for piece in range(3):
        pieces.append(lax.reduce_precision(scores, exponent_bits=8, mantissa_bits=7))
        scores = scores - pieces[-1]
    pieces = jnp.concatenate(pieces, axis=0).astype(jnp.bfloat16)
    count = pieces.shape[0]
    slots = TAIL * SHARE // local_rows
    pieces = jnp.pad(pieces, ((0, slots - count), (0, 0))).reshape(TAIL, SHARE)
    payload = jnp.concatenate([share, pieces], axis=0)
    near = lax.all_to_all(
        jnp.broadcast_to(payload, (rings,) + payload.shape), "y", 0, 0
    )
    own_share = near[:, :capacity].reshape(rings * capacity, SHARE)
    last = lax.all_gather(own_share, "tp", axis=0)

    tail = near[:, capacity:].reshape(rings, slots, local_rows)[:, :count]
    tail = jnp.sum(tail.reshape(rings, 3, experts, local_rows).astype(jnp.float32), axis=1)
    own = balance(jnp.stack([lax.axis_index("y"), owner]), tail, swap_cores(tail))

    start = prepare(last, w_gate, w_up, gate2, up2)
    start = pltpu.with_memory_space_constraint(start, pltpu.VMEM)
    own, start = lax.optimization_barrier((own, start))
    hidden = ffn(rows, w_gate, w_up, gate2, up2, start)
    full_hidden = lax.all_gather(hidden, "tp", axis=0)
    partial = down(full_hidden, w_down, down2)
    sums = lax.all_to_all(partial.reshape(rings, capacity, partial.shape[1]), "y", 0, 0)
    shares = weigh(sums, select, own)
    shares = lax.all_to_all(shares.reshape(owners, out_rows, shares.shape[1]), "exp", 0, 0)
    return jnp.sum(shares.astype(jnp.float32), axis=0).astype(jnp.bfloat16)


def solution(mesh):
    shape = mesh.devices.shape
    fine = Mesh(
        mesh.devices.reshape((shape[0] // CORES, CORES) + shape[1:]), ("y", "core", "exp", "tp")
    )
    tok = ("y", "core")
    placed = (
        P(tok, None),
        P(),
        P("exp", None, tok + ("tp",)),
        P("exp", None, tok + ("tp",)),
        P("exp", tok, "tp"),
        P(tok, None),
        P(tok, None),
    )
    return jax.shard_map(
        local, mesh=fine, in_specs=placed, out_specs=P(tok + ("exp",), "tp"), check_vma=False
    )
```

```python
import jax
import jax.numpy as jnp
from jax import lax
from jax.experimental import pallas as pl
from jax.experimental.pallas import tpu as pltpu
from jax.sharding import Mesh, PartitionSpec as P

TOP = 2
ITERS = 4
SOFT_CAP = 8.0
CORES = 2
ALL_VMEM = 64 << 20
FFN_VMEM = 60 << 20
SHARE = 256
TAIL = 16


def swap_cores(value):
    return lax.ppermute(value, "core", [(0, 1), (1, 0)])


def route_kernel(
    owner_ref, part_ref, limits_hbm, assign_hbm, tokens_hbm, select_ref, rows_hbm, share_ref,
    limits_ref, assign_ref, tokens_ref, own_ref, rows_ref, sems, out_sems
):
    width = tokens_ref.shape[1]
    share = own_ref.shape[1]
    chunks = out_sems.shape[0]
    parts = [pl.ds(index * (width // chunks), width // chunks) for index in range(chunks)]
    owner = owner_ref[0]
    first = pl.multiple_of(width + part_ref[0] * share, 128)
    small = [
        pltpu.make_async_copy(limits_hbm, limits_ref, sems.at[chunks]),
        pltpu.make_async_copy(assign_hbm, assign_ref, sems.at[chunks + 1]),
    ]
    copies = [
        pltpu.make_async_copy(tokens_hbm.at[:, part], tokens_ref.at[:, part], sems.at[index])
        for index, part in enumerate(parts)
    ]
    last = pltpu.make_async_copy(
        tokens_hbm.at[:, pl.ds(first, share)], own_ref, sems.at[chunks + 2]
    )
    for copy in small + copies + [last]:
        copy.start()
    capacity, count = select_ref.shape
    row = lax.broadcasted_iota(jnp.int32, (count, count), 0)
    column = lax.broadcasted_iota(jnp.int32, (count, count), 1)
    earlier = jnp.where(row < column, 1.0, 0.0).astype(jnp.bfloat16)
    slot_ids = lax.broadcasted_iota(jnp.int32, (capacity, count), 0)
    for copy in small:
        copy.wait()
    hit = jnp.sum(jnp.where(assign_ref[...] == owner, 1.0, 0.0), axis=0, keepdims=True)
    named = jnp.broadcast_to(hit, (16, count)).astype(jnp.bfloat16)
    slot = jnp.dot(named, earlier, preferred_element_type=jnp.float32)[:1].astype(jnp.int32)
    slot = jnp.where((hit > 0.0) & (slot < limits_ref[0, owner]), slot, -1)
    select = jnp.where(slot_ids == slot, 1.0, 0.0).astype(jnp.bfloat16)
    select_ref[...] = select
    outs = []
    for index, part in enumerate(parts):
        copies[index].wait()
        rows_ref[:, part] = jnp.dot(
            select, tokens_ref[:, part], preferred_element_type=jnp.float32
        ).astype(rows_ref.dtype)
        outs.append(
            pltpu.make_async_copy(
                rows_ref.at[:, part], rows_hbm.at[:, part], out_sems.at[index]
            )
        )
        outs[-1].start()
    last.wait()
    share_ref[...] = jnp.dot(
        select, own_ref[...], preferred_element_type=jnp.float32
    ).astype(share_ref.dtype)
    for copy in outs:
        copy.wait()


def route(owner, part, limits, assignments, tokens, capacity, share, parts, chunks=3):
    count = tokens.shape[0]
    width = tokens.shape[1] - parts * share
    far = pl.BlockSpec(memory_space=pltpu.HBM)
    near = pl.BlockSpec(memory_space=pltpu.VMEM)
    return pl.pallas_call(
        route_kernel,
        in_specs=[pl.BlockSpec(memory_space=pltpu.SMEM)] * 2 + [far] * 3,
        out_specs=[near, far, near],
        out_shape=[
            jax.ShapeDtypeStruct((capacity, count), jnp.bfloat16),
            jax.ShapeDtypeStruct((capacity, width), jnp.bfloat16),
            jax.ShapeDtypeStruct((capacity, share), jnp.bfloat16),
        ],
        scratch_shapes=[
            pltpu.SMEM(limits.shape, jnp.int32),
            pltpu.VMEM(assignments.shape, jnp.int32),
            pltpu.VMEM((count, width), jnp.bfloat16),
            pltpu.VMEM((count, share), jnp.bfloat16),
            pltpu.VMEM((capacity, width), jnp.bfloat16),
            pltpu.SemaphoreType.DMA((chunks + 3,)),
            pltpu.SemaphoreType.DMA((chunks,)),
        ],
        compiler_params=pltpu.CompilerParams(vmem_limit_bytes=ALL_VMEM),
        cost_estimate=pl.CostEstimate(
            flops=2 * capacity * count * (width + share),
            bytes_accessed=2 * (count + capacity) * (width + share),
            transcendentals=0,
        ),
        name="route",
    )(owner, part, limits, assignments, tokens)


def prepare_kernel(
    last_hbm, gate_hbm, up_hbm, gate2_hbm, up2_hbm, total_ref, last_ref, weight_ref, sems
):
    shares, _, share = last_ref.shape
    width, units = gate_hbm.shape
    tail = pl.ds(width - shares * share, shares * share)
    copies = [pltpu.make_async_copy(last_hbm, last_ref, sems.at[0])]
    for place, ref in enumerate((gate_hbm, up_hbm, gate2_hbm, up2_hbm)):
        copies.append(
            pltpu.make_async_copy(
                ref.at[tail, :], weight_ref.at[:, pl.ds(place * units, units)], sems.at[1 + place]
            )
        )
    for copy in copies:
        copy.start()
    for copy in copies:
        copy.wait()
    total = None
    for index in range(shares):
        product = jnp.dot(
            last_ref[index],
            weight_ref[pl.ds(index * share, share), :],
            preferred_element_type=jnp.float32,
        )
        total = product if index == 0 else total + product
    total_ref[...] = total


def prepare(last, gate, up, gate2, up2):
    shares, count, share = last.shape
    units = gate.shape[1]
    return pl.pallas_call(
        prepare_kernel,
        in_specs=[pl.BlockSpec(memory_space=pltpu.HBM)] * 5,
        out_specs=pl.BlockSpec(memory_space=pltpu.VMEM),
        out_shape=pltpu.VMEM((count, 4 * units), jnp.float32),
        scratch_shapes=[
            pltpu.VMEM(last.shape, jnp.bfloat16),
            pltpu.VMEM((shares * share, 4 * units), jnp.bfloat16),
            pltpu.SemaphoreType.DMA((5,)),
        ],
        compiler_params=pltpu.CompilerParams(vmem_limit_bytes=FFN_VMEM),
        cost_estimate=pl.CostEstimate(
            flops=8 * count * shares * share * units,
            bytes_accessed=2 * shares * share * (count + 4 * units) + 16 * count * units,
            transcendentals=0,
        ),
        name="prepare",
    )(last, gate, up, gate2, up2)


def ffn_kernel(
    rows_hbm, gate_hbm, up_hbm, gate2_hbm, up2_hbm, start_ref, out_ref, rows_ref, weight_ref, sems
):
    chunks, chunk, columns = weight_ref.shape
    units = columns // 4
    copies = []
    for index in range(chunks):
        part = pl.ds(index * chunk, chunk)
        ends = [(rows_hbm.at[:, part], rows_ref.at[index])]
        for place, ref in enumerate((gate_hbm, up_hbm, gate2_hbm, up2_hbm)):
            ends.append(
                (ref.at[part, :], weight_ref.at[index, :, pl.ds(place * units, units)])
            )
        copies.append(
            [
                pltpu.make_async_copy(source, sink, sems.at[index, place])
                for place, (source, sink) in enumerate(ends)
            ]
        )
    for group in copies:
        for copy in group:
            copy.start()
    total = start_ref[...]
    for index, group in enumerate(copies):
        for copy in group:
            copy.wait()
        total = total + jnp.dot(
            rows_ref[index], weight_ref[index], preferred_element_type=jnp.float32
        )
    for side in range(2):
        gate = total[:, 2 * side * units : (2 * side + 1) * units]
        up = total[:, (2 * side + 1) * units : (2 * side + 2) * units]
        hidden = gate / (1.0 + jnp.exp(-gate)) * up
        out_ref[:, side * units : (side + 1) * units] = hidden.astype(out_ref.dtype)


def ffn(rows, gate, up, gate2, up2, start, chunk=512):
    count, main = rows.shape
    units = gate.shape[1]
    near = pl.BlockSpec(memory_space=pltpu.VMEM)
    return pl.pallas_call(
        ffn_kernel,
        in_specs=[pl.BlockSpec(memory_space=pltpu.HBM)] * 5 + [near],
        out_specs=near,
        out_shape=pltpu.VMEM((count, 2 * units), jnp.bfloat16),
        scratch_shapes=[
            pltpu.VMEM((main // chunk, count, chunk), jnp.bfloat16),
            pltpu.VMEM((main // chunk, chunk, 4 * units), jnp.bfloat16),
            pltpu.SemaphoreType.DMA((main // chunk, 5)),
        ],
        compiler_params=pltpu.CompilerParams(vmem_limit_bytes=FFN_VMEM),
        cost_estimate=pl.CostEstimate(
            flops=8 * count * main * units,
            bytes_accessed=2 * count * main + 8 * main * units,
            transcendentals=2 * count * units,
        ),
        name="ffn",
    )(rows, gate, up, gate2, up2, start)


def down_kernel(hidden_ref, down_ref, down2_ref, out_hbm, out_ref, sems):
    parts = hidden_ref.shape[0]
    units = down_ref.shape[0] // parts
    chunks, _, chunk = out_ref.shape
    copies = []
    for place in range(chunks):
        column = pl.ds(place * chunk, chunk)
        total = None
        for index in range(parts):
            part = pl.ds(index * units, units)
            both = jnp.concatenate([down_ref[part, column], down2_ref[part, column]], axis=0)
            product = jnp.dot(hidden_ref[index], both, preferred_element_type=jnp.float32)
            total = product if index == 0 else total + product
        out_ref[place] = total.astype(out_ref.dtype)
        copies.append(
            pltpu.make_async_copy(out_ref.at[place], out_hbm.at[:, column], sems.at[place])
        )
        copies[-1].start()
    for copy in copies:
        copy.wait()


def down(hidden, weight, weight2, chunks=4):
    parts, count, units = hidden.shape
    columns = weight.shape[1]
    near = pl.BlockSpec(memory_space=pltpu.VMEM)
    return pl.pallas_call(
        down_kernel,
        in_specs=[near] * 3,
        out_specs=pl.BlockSpec(memory_space=pltpu.HBM),
        out_shape=jax.ShapeDtypeStruct((count, columns), jnp.bfloat16),
        scratch_shapes=[
            pltpu.VMEM((chunks, count, columns // chunks), jnp.bfloat16),
            pltpu.SemaphoreType.DMA((chunks,)),
        ],
        compiler_params=pltpu.CompilerParams(vmem_limit_bytes=24 << 20),
        cost_estimate=pl.CostEstimate(
            flops=2 * parts * count * units * columns,
            bytes_accessed=2 * parts * units * (count + columns) + 2 * count * columns,
            transcendentals=0,
        ),
        name="down",
    )(hidden, weight, weight2)


def weigh_kernel(parts_ref, select_ref, gate_ref, out_ref):
    select = select_ref[...]
    total = jnp.sum(parts_ref[...].astype(jnp.float32), axis=0).astype(jnp.bfloat16)
    gate = jnp.sum(select.astype(jnp.float32) * gate_ref[...], axis=1, keepdims=True)
    weighted = (total.astype(jnp.float32) * gate).astype(jnp.bfloat16)
    out_ref[...] = lax.dot_general(
        select, weighted, (((0,), (0,)), ((), ())), preferred_element_type=jnp.float32
    ).astype(out_ref.dtype)


def weigh(parts, select, gate):
    count = select.shape[1]
    columns = parts.shape[2]
    return pl.pallas_call(
        weigh_kernel,
        out_shape=jax.ShapeDtypeStruct((count, columns), jnp.bfloat16),
        compiler_params=pltpu.CompilerParams(vmem_limit_bytes=24 << 20),
        cost_estimate=pl.CostEstimate(
            flops=2 * count * select.shape[0] * columns,
            bytes_accessed=2 * parts.size + 2 * count * columns,
            transcendentals=0,
        ),
        name="weigh",
    )(parts, select, gate)


def local(tokens, router_weight, gate_weight, up_weight, down_weight, assignments, limits):
    local_rows = tokens.shape[0]
    experts = router_weight.shape[1]
    rings = lax.axis_size("y")
    shards = rings * CORES
    owners = lax.axis_size("exp")
    parts = lax.axis_size("tp")
    capacity = min(local_rows, max(2, 3 * local_rows * TOP // (2 * experts)))
    out_rows = local_rows // owners
    target = local_rows * shards * TOP / experts
    owner = lax.axis_index("exp")

    place = [jnp.reshape(lax.axis_index(axis), (1,)) for axis in ("exp", "tp")]
    select, main, share = route(*place, limits, assignments.T, tokens, capacity, SHARE, parts)
    rows = lax.all_gather(main, "y", axis=0, tiled=True)

    w_gate, w_up, w_down, tokens2, share, _ = lax.optimization_barrier(
        (gate_weight[0], up_weight[0], down_weight[0], tokens, share, main)
    )
    gate2, up2, down2 = swap_cores(w_gate), swap_cores(w_up), swap_cores(w_down)
    logits = lax.dot_general(
        router_weight, tokens2, (((0,), (1,)), ((), ())), preferred_element_type=jnp.float32
    )
    scores = SOFT_CAP * jnp.tanh(logits / SOFT_CAP)
    pieces = []
    for piece in range(3):
        pieces.append(lax.reduce_precision(scores, exponent_bits=8, mantissa_bits=7))
        scores = scores - pieces[-1]
    pieces = jnp.concatenate(pieces, axis=0).astype(jnp.bfloat16)
    count = pieces.shape[0]
    slots = TAIL * SHARE // local_rows
    pieces = jnp.pad(pieces, ((0, slots - count), (0, 0))).reshape(TAIL, SHARE)
    payload = jnp.concatenate([share, pieces], axis=0)
    near = lax.all_to_all(
        jnp.broadcast_to(payload, (rings,) + payload.shape), "y", 0, 0
    )
    own_share = near[:, :capacity].reshape(rings * capacity, SHARE)
    last = lax.all_gather(own_share, "tp", axis=0)

    tail = near[:, capacity:].reshape(rings, slots, local_rows)[:, :count]
    tail = jnp.sum(tail.reshape(rings, 3, experts, local_rows).astype(jnp.float32), axis=1)
    weights = jnp.exp(jnp.concatenate([tail, swap_cores(tail)], axis=0))
    weights = weights * (TOP / jnp.sum(weights, axis=1, keepdims=True))
    for repeat in range(ITERS):
        weights = weights * (target / jnp.sum(weights, axis=(0, 2), keepdims=True))
        weights = weights * (TOP / jnp.sum(weights, axis=1, keepdims=True))
    own = lax.dynamic_slice(weights, (lax.axis_index("y"), owner, 0), (1, 1, local_rows))[0]

    start = prepare(last, w_gate, w_up, gate2, up2)
    start = pltpu.with_memory_space_constraint(start, pltpu.VMEM)
    hidden = ffn(rows, w_gate, w_up, gate2, up2, start)
    full_hidden = lax.all_gather(hidden, "tp", axis=0)
    partial = down(full_hidden, w_down, down2)
    sums = lax.all_to_all(partial.reshape(rings, capacity, partial.shape[1]), "y", 0, 0)
    shares = weigh(sums, select, own)
    shares = lax.all_to_all(shares.reshape(owners, out_rows, shares.shape[1]), "exp", 0, 0)
    return jnp.sum(shares.astype(jnp.float32), axis=0).astype(jnp.bfloat16)


def solution(mesh):
    shape = mesh.devices.shape
    fine = Mesh(
        mesh.devices.reshape((shape[0] // CORES, CORES) + shape[1:]), ("y", "core", "exp", "tp")
    )
    tok = ("y", "core")
    placed = (
        P(tok, None),
        P(),
        P("exp", None, tok + ("tp",)),
        P("exp", None, tok + ("tp",)),
        P("exp", tok, "tp"),
        P(tok, None),
        P(tok, None),
    )
    return jax.shard_map(
        local, mesh=fine, in_specs=placed, out_specs=P(tok + ("exp",), "tp"), check_vma=False
    )
```

```python
import jax
import jax.numpy as jnp
from jax import lax
from jax.experimental import pallas as pl
from jax.experimental.pallas import tpu as pltpu
from jax.sharding import Mesh, PartitionSpec as P

TOP = 2
ITERS = 4
SOFT_CAP = 8.0
CORES = 2
ALL_VMEM = 64 << 20
FFN_VMEM = 60 << 20
SHARE = 256
TAIL = 16


def swap_cores(value):
    return lax.ppermute(value, "core", [(0, 1), (1, 0)])


def route_kernel(
    owner_ref, part_ref, limits_hbm, assign_hbm, tokens_hbm, select_ref, rows_hbm, share_ref,
    limits_ref, assign_ref, tokens_ref, own_ref, rows_ref, sems, out_sems
):
    width = tokens_ref.shape[1]
    share = own_ref.shape[1]
    chunks = out_sems.shape[0]
    parts = [pl.ds(index * (width // chunks), width // chunks) for index in range(chunks)]
    owner = owner_ref[0]
    first = pl.multiple_of(width + part_ref[0] * share, 128)
    small = [
        pltpu.make_async_copy(limits_hbm, limits_ref, sems.at[chunks]),
        pltpu.make_async_copy(assign_hbm, assign_ref, sems.at[chunks + 1]),
    ]
    copies = [
        pltpu.make_async_copy(tokens_hbm.at[:, part], tokens_ref.at[:, part], sems.at[index])
        for index, part in enumerate(parts)
    ]
    last = pltpu.make_async_copy(
        tokens_hbm.at[:, pl.ds(first, share)], own_ref, sems.at[chunks + 2]
    )
    for copy in small + copies + [last]:
        copy.start()
    capacity, count = select_ref.shape
    row = lax.broadcasted_iota(jnp.int32, (count, count), 0)
    column = lax.broadcasted_iota(jnp.int32, (count, count), 1)
    earlier = jnp.where(row < column, 1.0, 0.0).astype(jnp.bfloat16)
    slot_ids = lax.broadcasted_iota(jnp.int32, (capacity, count), 0)
    for copy in small:
        copy.wait()
    hit = jnp.sum(jnp.where(assign_ref[...] == owner, 1.0, 0.0), axis=0, keepdims=True)
    named = jnp.broadcast_to(hit, (16, count)).astype(jnp.bfloat16)
    slot = jnp.dot(named, earlier, preferred_element_type=jnp.float32)[:1].astype(jnp.int32)
    slot = jnp.where((hit > 0.0) & (slot < limits_ref[0, owner]), slot, -1)
    select = jnp.where(slot_ids == slot, 1.0, 0.0).astype(jnp.bfloat16)
    select_ref[...] = select
    outs = []
    for index, part in enumerate(parts):
        copies[index].wait()
        rows_ref[:, part] = jnp.dot(
            select, tokens_ref[:, part], preferred_element_type=jnp.float32
        ).astype(rows_ref.dtype)
        outs.append(
            pltpu.make_async_copy(
                rows_ref.at[:, part], rows_hbm.at[:, part], out_sems.at[index]
            )
        )
        outs[-1].start()
    last.wait()
    share_ref[...] = jnp.dot(
        select, own_ref[...], preferred_element_type=jnp.float32
    ).astype(share_ref.dtype)
    for copy in outs:
        copy.wait()


def route(owner, part, limits, assignments, tokens, capacity, share, parts, chunks=3):
    count = tokens.shape[0]
    width = tokens.shape[1] - parts * share
    far = pl.BlockSpec(memory_space=pltpu.HBM)
    near = pl.BlockSpec(memory_space=pltpu.VMEM)
    return pl.pallas_call(
        route_kernel,
        in_specs=[pl.BlockSpec(memory_space=pltpu.SMEM)] * 2 + [far] * 3,
        out_specs=[near, far, near],
        out_shape=[
            jax.ShapeDtypeStruct((capacity, count), jnp.bfloat16),
            jax.ShapeDtypeStruct((capacity, width), jnp.bfloat16),
            jax.ShapeDtypeStruct((capacity, share), jnp.bfloat16),
        ],
        scratch_shapes=[
            pltpu.SMEM(limits.shape, jnp.int32),
            pltpu.VMEM(assignments.shape, jnp.int32),
            pltpu.VMEM((count, width), jnp.bfloat16),
            pltpu.VMEM((count, share), jnp.bfloat16),
            pltpu.VMEM((capacity, width), jnp.bfloat16),
            pltpu.SemaphoreType.DMA((chunks + 3,)),
            pltpu.SemaphoreType.DMA((chunks,)),
        ],
        compiler_params=pltpu.CompilerParams(vmem_limit_bytes=ALL_VMEM),
        cost_estimate=pl.CostEstimate(
            flops=2 * capacity * count * (width + share),
            bytes_accessed=2 * (count + capacity) * (width + share),
            transcendentals=0,
        ),
        name="route",
    )(owner, part, limits, assignments, tokens)


def prepare_kernel(
    last_hbm, gate_hbm, up_hbm, gate2_hbm, up2_hbm, total_ref, last_ref, weight_ref, sems
):
    shares, _, share = last_ref.shape
    width, units = gate_hbm.shape
    tail = pl.ds(width - shares * share, shares * share)
    copies = [pltpu.make_async_copy(last_hbm, last_ref, sems.at[0])]
    for place, ref in enumerate((gate_hbm, up_hbm, gate2_hbm, up2_hbm)):
        copies.append(
            pltpu.make_async_copy(
                ref.at[tail, :], weight_ref.at[:, pl.ds(place * units, units)], sems.at[1 + place]
            )
        )
    for copy in copies:
        copy.start()
    for copy in copies:
        copy.wait()
    total = None
    for index in range(shares):
        product = jnp.dot(
            last_ref[index],
            weight_ref[pl.ds(index * share, share), :],
            preferred_element_type=jnp.float32,
        )
        total = product if index == 0 else total + product
    total_ref[...] = total


def prepare(last, gate, up, gate2, up2):
    shares, count, share = last.shape
    units = gate.shape[1]
    return pl.pallas_call(
        prepare_kernel,
        in_specs=[pl.BlockSpec(memory_space=pltpu.HBM)] * 5,
        out_specs=pl.BlockSpec(memory_space=pltpu.VMEM),
        out_shape=pltpu.VMEM((count, 4 * units), jnp.float32),
        scratch_shapes=[
            pltpu.VMEM(last.shape, jnp.bfloat16),
            pltpu.VMEM((shares * share, 4 * units), jnp.bfloat16),
            pltpu.SemaphoreType.DMA((5,)),
        ],
        compiler_params=pltpu.CompilerParams(vmem_limit_bytes=FFN_VMEM),
        cost_estimate=pl.CostEstimate(
            flops=8 * count * shares * share * units,
            bytes_accessed=2 * shares * share * (count + 4 * units) + 16 * count * units,
            transcendentals=0,
        ),
        name="prepare",
    )(last, gate, up, gate2, up2)


def ffn_kernel(
    rows_hbm, gate_hbm, up_hbm, gate2_hbm, up2_hbm, start_ref, out_ref, rows_ref, weight_ref, sems
):
    chunks, chunk, columns = weight_ref.shape
    units = columns // 4
    copies = []
    for index in range(chunks):
        part = pl.ds(index * chunk, chunk)
        ends = [(rows_hbm.at[:, part], rows_ref.at[index])]
        for place, ref in enumerate((gate_hbm, up_hbm, gate2_hbm, up2_hbm)):
            ends.append(
                (ref.at[part, :], weight_ref.at[index, :, pl.ds(place * units, units)])
            )
        copies.append(
            [
                pltpu.make_async_copy(source, sink, sems.at[index, place])
                for place, (source, sink) in enumerate(ends)
            ]
        )
    for group in copies:
        for copy in group:
            copy.start()
    total = start_ref[...]
    for index, group in enumerate(copies):
        for copy in group:
            copy.wait()
        total = total + jnp.dot(
            rows_ref[index], weight_ref[index], preferred_element_type=jnp.float32
        )
    for side in range(2):
        gate = total[:, 2 * side * units : (2 * side + 1) * units]
        up = total[:, (2 * side + 1) * units : (2 * side + 2) * units]
        hidden = gate / (1.0 + jnp.exp(-gate)) * up
        out_ref[:, side * units : (side + 1) * units] = hidden.astype(out_ref.dtype)


def ffn(rows, gate, up, gate2, up2, start, chunk=256):
    count, main = rows.shape
    units = gate.shape[1]
    near = pl.BlockSpec(memory_space=pltpu.VMEM)
    return pl.pallas_call(
        ffn_kernel,
        in_specs=[pl.BlockSpec(memory_space=pltpu.HBM)] * 5 + [near],
        out_specs=near,
        out_shape=pltpu.VMEM((count, 2 * units), jnp.bfloat16),
        scratch_shapes=[
            pltpu.VMEM((main // chunk, count, chunk), jnp.bfloat16),
            pltpu.VMEM((main // chunk, chunk, 4 * units), jnp.bfloat16),
            pltpu.SemaphoreType.DMA((main // chunk, 5)),
        ],
        compiler_params=pltpu.CompilerParams(vmem_limit_bytes=FFN_VMEM),
        cost_estimate=pl.CostEstimate(
            flops=8 * count * main * units,
            bytes_accessed=2 * count * main + 8 * main * units,
            transcendentals=2 * count * units,
        ),
        name="ffn",
    )(rows, gate, up, gate2, up2, start)


def down_kernel(hidden_ref, down_ref, down2_ref, out_ref):
    parts = hidden_ref.shape[0]
    units = down_ref.shape[0] // parts
    total = None
    for index in range(parts):
        part = pl.ds(index * units, units)
        both = jnp.concatenate([down_ref[part, :], down2_ref[part, :]], axis=0)
        product = jnp.dot(hidden_ref[index], both, preferred_element_type=jnp.float32)
        total = product if index == 0 else total + product
    out_ref[...] = total.astype(out_ref.dtype)


def down(hidden, weight, weight2):
    parts, count, units = hidden.shape
    columns = weight.shape[1]
    return pl.pallas_call(
        down_kernel,
        out_shape=pltpu.VMEM((count, columns), jnp.bfloat16),
        compiler_params=pltpu.CompilerParams(vmem_limit_bytes=24 << 20),
        cost_estimate=pl.CostEstimate(
            flops=2 * parts * count * units * columns,
            bytes_accessed=2 * parts * units * (count + columns) + 2 * count * columns,
            transcendentals=0,
        ),
        name="down",
    )(hidden, weight, weight2)


def weigh_kernel(parts_ref, select_ref, gate_ref, out_ref):
    select = select_ref[...]
    total = jnp.sum(parts_ref[...].astype(jnp.float32), axis=0).astype(jnp.bfloat16)
    gate = jnp.sum(select.astype(jnp.float32) * gate_ref[...], axis=1, keepdims=True)
    weighted = (total.astype(jnp.float32) * gate).astype(jnp.bfloat16)
    out_ref[...] = lax.dot_general(
        select, weighted, (((0,), (0,)), ((), ())), preferred_element_type=jnp.float32
    ).astype(out_ref.dtype)


def weigh(parts, select, gate):
    count = select.shape[1]
    columns = parts.shape[2]
    return pl.pallas_call(
        weigh_kernel,
        out_shape=jax.ShapeDtypeStruct((count, columns), jnp.bfloat16),
        compiler_params=pltpu.CompilerParams(vmem_limit_bytes=24 << 20),
        cost_estimate=pl.CostEstimate(
            flops=2 * count * select.shape[0] * columns,
            bytes_accessed=2 * parts.size + 2 * count * columns,
            transcendentals=0,
        ),
        name="weigh",
    )(parts, select, gate)


def local(tokens, router_weight, gate_weight, up_weight, down_weight, assignments, limits):
    local_rows = tokens.shape[0]
    experts = router_weight.shape[1]
    rings = lax.axis_size("y")
    shards = rings * CORES
    owners = lax.axis_size("exp")
    parts = lax.axis_size("tp")
    capacity = min(local_rows, max(2, 3 * local_rows * TOP // (2 * experts)))
    out_rows = local_rows // owners
    target = local_rows * shards * TOP / experts
    owner = lax.axis_index("exp")

    place = [jnp.reshape(lax.axis_index(axis), (1,)) for axis in ("exp", "tp")]
    select, main, share = route(*place, limits, assignments.T, tokens, capacity, SHARE, parts)
    rows = lax.all_gather(main, "y", axis=0, tiled=True)

    w_gate, w_up, w_down, tokens2, share, _ = lax.optimization_barrier(
        (gate_weight[0], up_weight[0], down_weight[0], tokens, share, main)
    )
    gate2, up2, down2 = swap_cores(w_gate), swap_cores(w_up), swap_cores(w_down)
    logits = lax.dot_general(
        router_weight, tokens2, (((0,), (1,)), ((), ())), preferred_element_type=jnp.float32
    )
    scores = SOFT_CAP * jnp.tanh(logits / SOFT_CAP)
    pieces = []
    for piece in range(3):
        pieces.append(lax.reduce_precision(scores, exponent_bits=8, mantissa_bits=7))
        scores = scores - pieces[-1]
    pieces = jnp.concatenate(pieces, axis=0).astype(jnp.bfloat16)
    count = pieces.shape[0]
    slots = TAIL * SHARE // local_rows
    pieces = jnp.pad(pieces, ((0, slots - count), (0, 0))).reshape(TAIL, SHARE)
    payload = jnp.concatenate([share, pieces], axis=0)
    near = lax.all_to_all(
        jnp.broadcast_to(payload, (rings,) + payload.shape), "y", 0, 0
    )
    own_share = near[:, :capacity].reshape(rings * capacity, SHARE)
    last = lax.all_gather(own_share, "tp", axis=0)

    tail = near[:, capacity:].reshape(rings, slots, local_rows)[:, :count]
    tail = jnp.sum(tail.reshape(rings, 3, experts, local_rows).astype(jnp.float32), axis=1)
    weights = jnp.exp(jnp.concatenate([tail, swap_cores(tail)], axis=0))
    weights = weights * (TOP / jnp.sum(weights, axis=1, keepdims=True))
    for repeat in range(ITERS):
        weights = weights * (target / jnp.sum(weights, axis=(0, 2), keepdims=True))
        weights = weights * (TOP / jnp.sum(weights, axis=1, keepdims=True))
    own = lax.dynamic_slice(weights, (lax.axis_index("y"), owner, 0), (1, 1, local_rows))[0]

    start = prepare(last, w_gate, w_up, gate2, up2)
    start = pltpu.with_memory_space_constraint(start, pltpu.VMEM)
    hidden = ffn(rows, w_gate, w_up, gate2, up2, start)
    full_hidden = lax.all_gather(hidden, "tp", axis=0)
    partial = down(full_hidden, w_down, down2)
    sums = lax.all_to_all(partial.reshape(rings, capacity, partial.shape[1]), "y", 0, 0)
    shares = weigh(sums, select, own)
    shares = lax.all_to_all(shares.reshape(owners, out_rows, shares.shape[1]), "exp", 0, 0)
    return jnp.sum(shares.astype(jnp.float32), axis=0).astype(jnp.bfloat16)


def solution(mesh):
    shape = mesh.devices.shape
    fine = Mesh(
        mesh.devices.reshape((shape[0] // CORES, CORES) + shape[1:]), ("y", "core", "exp", "tp")
    )
    tok = ("y", "core")
    placed = (
        P(tok, None),
        P(),
        P("exp", None, tok + ("tp",)),
        P("exp", None, tok + ("tp",)),
        P("exp", tok, "tp"),
        P(tok, None),
        P(tok, None),
    )
    return jax.shard_map(
        local, mesh=fine, in_specs=placed, out_specs=P(tok + ("exp",), "tp"), check_vma=False
    )
```
